32 devices in a mesh: leaf: 8 (over z, y), rhs: 4 (over x, core).
Axes of the slice: x: 2, y: 2, z: 4, core: 2. Of those that a mesh axis runs over, the one named last changes fastest.
Arguments:
- leaf_rhs: bfloat16 [1024, 8192], P('rhs', 'leaf'), parts along dimension 0, may hold values from -6 to 6
- sep_rhs: bfloat16 [1024, 2048], P('rhs', 'leaf'), parts along dimension 0, may hold values from -6 to 6
- leaf_inverse: bfloat16 [8192, 1024], P('leaf'), may hold values from -1.4 to 1.4, as said below
- leaf_update: bfloat16 [8, 3, 1024, 128], P('leaf'), may hold values from -1 to 1
- leaf_panel: int32 [8, 3], P('leaf'), may hold values from 0 to 1
- sep_inverse: bfloat16 [2048, 256], P('leaf'), may hold values from -1.4 to 1.4, as said below
- sep_update: bfloat16 [8, 3, 256, 128], P('leaf'), may hold values from -1 to 1
- sep_panel: int32 [8, 3], P('leaf'), may hold values from 0 to 1
Outputs:
- leaf_solution: float32 [1024, 8192], P('rhs', 'leaf'), parts along dimension 0
- sep_solution: float32 [1024, 2048], P('rhs', 'leaf'), parts along dimension 0
The draws below stay inside these ranges and needn't reach their ends.
There are 4 independent parts, one for each index of `rhs`. The reference program is written for one: setup_inputs(seed, part) draws one part's arguments, and reference() takes and returns one part's arrays. A program takes and returns all parts, laid end to end along the dimension named above; an argument that names none is the same for every part. Nothing has to cross between parts.
Inputs may be any that keep to these rules, and one draw needn't show every extreme that they name: `leaf_inverse`: each diagonal 1024 x 1024 block is lower triangular with diagonal entries between 0.6 and 1.4. `sep_inverse`: each diagonal 256 x 256 block is lower triangular with diagonal entries between 0.6 and 1.4.
All inputs are finite; a program needn't handle non-finite values.
Results may differ from the reference program's by a relative error of at most 0.0047.
Values may be sent and summed in bfloat16 or wider, within the bound.
No kernel may reach another device: no remote copies, remote signals or barrier semaphores. Data moves between devices by JAX's collectives and lax.ppermute only.
A program may use at most 64 MiB of HBM per device.

```python
import math
import jax
import jax.numpy as jnp
from jax import lax

LEAF_ROWS = 1024
SEP = 256
PANEL = 128
RHS = 256
NODES = 8
LEVELS = 3


def lower_factor(key, order):
    row_pos = jnp.arange(NODES * order, dtype=jnp.int32)[:, None] % order
    col_pos = jnp.arange(order, dtype=jnp.int32)[None, :]
    first_key, second_key = jax.random.split(key)
    diagonal = jax.random.uniform(first_key, (NODES * order, order), jnp.float32, 0.6, 1.4)
    below = jnp.clip(jax.random.normal(second_key, (NODES * order, order), jnp.float32), -4.0, 4.0) * (0.7 / math.sqrt(order))
    value = jnp.where(row_pos == col_pos, diagonal, jnp.where(col_pos < row_pos, below, 0.0))
    return value.astype(jnp.bfloat16)


def ancestor_blocks(key, order):
    tier = jnp.arange(LEVELS, dtype=jnp.float32)[None, :, None, None]
    factor = jnp.exp2(-0.5 * (tier + 1.0)) / math.sqrt(order)
    value = jnp.clip(jax.random.normal(key, (NODES, LEVELS, order, PANEL), jnp.float32), -4.0, 4.0) * factor
    return value.astype(jnp.bfloat16)


def draw_leaf_inverse(key, part):
    return lower_factor(jax.random.fold_in(key, 11), LEAF_ROWS)


def draw_sep_inverse(key, part):
    return lower_factor(jax.random.fold_in(key, 23), SEP)


def draw_leaf_update(key, part):
    return ancestor_blocks(jax.random.fold_in(key, 37), LEAF_ROWS)


def draw_sep_update(key, part):
    return ancestor_blocks(jax.random.fold_in(key, 41), SEP)


def touch_ends(values, rng, smallest, top_value):
    longest = values.shape.index(max(values.shape))
    spots = []
    for shift in (0, 1):
        where = [jax.random.randint(jax.random.fold_in(rng, axis), (), 0, length) for axis, length in enumerate(values.shape)]
        where[longest] = (where[longest] + shift) % values.shape[longest]
        spots.append(tuple(where))
    return values.at[spots[0]].set(smallest).at[spots[1]].set(top_value)


def block_levels(key, dims, pieces, least, top_value):
    loudness, own = 1.0, jax.random.fold_in(key, 6)
    for position, parts in pieces:
        steps = jnp.exp(jax.random.uniform(jax.random.fold_in(own, position), (parts,), jnp.float32, least / len(pieces), top_value / len(pieces)))
        loudness = loudness * jnp.repeat(steps, dims[position] // parts).reshape([-1 if axis == position else 1 for axis in range(len(dims))])
    return loudness


def bell_draw(stream_key, shape, width, limit, cuts=(), held_as=jnp.bfloat16):
    entries = width * jax.random.normal(stream_key, shape, jnp.float32)
    if cuts:
        entries = entries * block_levels(stream_key, shape, cuts, -0.22, 0.18)
    return jnp.clip(entries, -limit, limit).astype(held_as)


def setup_inputs(seed: int = 0, part: int = 0) -> dict:
    arg_keys = jax.random.split(jax.random.key(seed), 9)
    part_keys = jax.random.split(jax.random.fold_in(arg_keys[8], part), 9)
    leaf_rhs = bell_draw(part_keys[0], (RHS, NODES * LEAF_ROWS), 1.0, 6.0, ((1, 8),))
    sep_rhs = bell_draw(part_keys[1], (RHS, NODES * SEP), 1.0, 6.0, ((1, 8),))
    leaf_inverse = draw_leaf_inverse(jax.random.fold_in(arg_keys[8], 71), part)
    leaf_update = draw_leaf_update(jax.random.fold_in(arg_keys[8], 71), part)
    leaf_panel = touch_ends(jax.random.randint(arg_keys[4], (NODES, LEVELS), 0, SEP // PANEL), jax.random.fold_in(arg_keys[4], 1), 0, (SEP // PANEL) - 1).astype(jnp.int32)
    sep_inverse = draw_sep_inverse(jax.random.fold_in(arg_keys[8], 71), part)
    sep_update = draw_sep_update(jax.random.fold_in(arg_keys[8], 71), part)
    sep_panel = touch_ends(jax.random.randint(arg_keys[7], (NODES, LEVELS), 0, SEP // PANEL), jax.random.fold_in(arg_keys[7], 1), 0, (SEP // PANEL) - 1).astype(jnp.int32)
    return dict(leaf_rhs=leaf_rhs, sep_rhs=sep_rhs, leaf_inverse=leaf_inverse, leaf_update=leaf_update, leaf_panel=leaf_panel, sep_inverse=sep_inverse, sep_update=sep_update, sep_panel=sep_panel)


def rounded_copy(vectors):
    return lax.optimization_barrier(vectors.astype(jnp.bfloat16)).astype(jnp.float32)


def place_updates(updates, segment_ids, groups, panel_count):
    summed = jax.ops.segment_sum(updates, segment_ids, num_segments=groups * panel_count)
    summed = summed.reshape(groups, panel_count, updates.shape[1], updates.shape[2])
    return jnp.transpose(summed, (0, 2, 1, 3)).reshape(groups, updates.shape[1], panel_count * updates.shape[2])


def pull_updates(rounded_vectors, rows_above, panel_ids, weights):
    panel_count = SEP // PANEL
    divided = rounded_vectors.reshape(rounded_vectors.shape[0], RHS, panel_count, PANEL)
    picked = divided[rows_above, :, panel_ids, :]
    return jnp.einsum("jrp,jsp->jrs", picked, weights.astype(jnp.float32), precision=lax.Precision.HIGHEST)


def owners_of(tree_level):
    groups = NODES >> (tree_level + 1)
    return jnp.arange(groups, dtype=jnp.int32) * (2 ** (tree_level + 1)) + (2 ** tree_level - 1)


def reference(leaf_rhs, sep_rhs, leaf_inverse, leaf_update, leaf_panel, sep_inverse, sep_update, sep_panel):
    highest = lax.Precision.HIGHEST
    panel_count = SEP // PANEL
    node_ids = jnp.arange(NODES, dtype=jnp.int32)
    leaf_vectors = jnp.transpose(leaf_rhs.reshape(RHS, NODES, LEAF_ROWS), (1, 0, 2)).astype(jnp.float32)
    leaf_matrices = leaf_inverse.reshape(NODES, LEAF_ROWS, LEAF_ROWS).astype(jnp.float32)
    leaf_solved = jnp.einsum("nrj,nij->nri", leaf_vectors, leaf_matrices, precision=highest)
    leaf_rounded = rounded_copy(leaf_solved)
    pending = []
    for tree_level in range(LEVELS):
        groups = NODES >> (tree_level + 1)
        updates = jnp.einsum("nrb,nbp->nrp", leaf_rounded, leaf_update[:, tree_level].astype(jnp.float32), precision=highest)
        segment_ids = (node_ids >> (tree_level + 1)) * panel_count + leaf_panel[:, tree_level]
        pending.append(place_updates(updates, segment_ids, groups, panel_count))
    sep_vectors = jnp.transpose(sep_rhs.reshape(RHS, NODES, SEP), (1, 0, 2)).astype(jnp.float32)
    sep_matrices = sep_inverse.reshape(NODES, SEP, SEP)
    solved_levels = []
    for tree_level in range(LEVELS):
        owners = owners_of(tree_level)
        residual = sep_vectors[owners] - pending[tree_level]
        inverse = sep_matrices[owners].astype(jnp.float32)
        solved = jnp.einsum("jrk,jik->jri", rounded_copy(residual), inverse, precision=highest)
        solved_rounded = rounded_copy(solved)
        for ancestor in range(tree_level + 1, LEVELS):
            updates = jnp.einsum("jrs,jsp->jrp", solved_rounded, sep_update[owners, ancestor].astype(jnp.float32), precision=highest)
            segment_ids = (owners >> (ancestor + 1)) * panel_count + sep_panel[owners, ancestor]
            pending[ancestor] = pending[ancestor] + place_updates(updates, segment_ids, NODES >> (ancestor + 1), panel_count)
        solved_levels.append(solved)
    rounded_levels = [None] * LEVELS
    sep_out = jnp.zeros((NODES, RHS, SEP), jnp.float32)
    for tree_level in reversed(range(LEVELS)):
        owners = owners_of(tree_level)
        gathered = jnp.zeros((owners.shape[0], RHS, SEP), jnp.float32)
        for ancestor in range(tree_level + 1, LEVELS):
            gathered = gathered + pull_updates(rounded_levels[ancestor], owners >> (ancestor + 1), sep_panel[owners, ancestor], sep_update[owners, ancestor])
        residual = solved_levels[tree_level] - gathered
        solution = jnp.einsum("jrk,jki->jri", rounded_copy(residual), sep_matrices[owners].astype(jnp.float32), precision=highest)
        rounded_levels[tree_level] = rounded_copy(solution)
        sep_out = sep_out.at[owners].set(solution)
    gathered = jnp.zeros((NODES, RHS, LEAF_ROWS), jnp.float32)
    for ancestor in range(LEVELS):
        gathered = gathered + pull_updates(rounded_levels[ancestor], node_ids >> (ancestor + 1), leaf_panel[:, ancestor], leaf_update[:, ancestor])
    leaf_out = jnp.einsum("nrk,nki->nri", rounded_copy(leaf_solved - gathered), leaf_matrices, precision=highest)
    leaf_solution = jnp.transpose(leaf_out, (1, 0, 2)).reshape(RHS, NODES * LEAF_ROWS)
    sep_solution = jnp.transpose(sep_out, (1, 0, 2)).reshape(RHS, NODES * SEP)
    return (leaf_solution, sep_solution)
```

```python
from functools import partial

import jax
import jax.numpy as jnp
from jax import lax
from jax.experimental import pallas as pl
from jax.experimental.pallas import tpu as pltpu
from jax.sharding import PartitionSpec as P

NOTE_ROWS = 16
f32, bf16 = jnp.float32, jnp.bfloat16


def dot(a, b):
    return jnp.dot(a, b, preferred_element_type=f32)


def dot_t(a, b):
    return lax.dot_general(a, b, (((1,), (1,)), ((), ())), preferred_element_type=f32)


def own_level(k, levels):
    level = jnp.int32(0)
    for bit in range(levels):
        low = (2 << bit) - 1
        level = jnp.where((k & low) == low, bit + 1, level)
    return level


def placed(block, panel, count):
    return jnp.concatenate(
        [jnp.where(panel == p, block, jnp.zeros_like(block)) for p in range(count)], axis=1
    )


def picked(vectors, panel, count):
    width = vectors.shape[1] // count
    result = vectors[:, :width]
    for p in range(1, count):
        result = jnp.where(panel == p, vectors[:, p * width : (p + 1) * width], result)
    return result


def call(kernel, outs, args, smem=(), flops=0):
    def bytes_of(arrays):
        return sum(a.size * a.dtype.itemsize for a in arrays)

    outs = [jax.ShapeDtypeStruct(shape, dtype) for shape, dtype in outs]
    return pl.pallas_call(
        kernel,
        out_shape=outs,
        in_specs=[
            pl.BlockSpec(memory_space=pltpu.SMEM if i in smem else pltpu.VMEM)
            for i in range(len(args))
        ],
        out_specs=[pl.BlockSpec(memory_space=pltpu.VMEM) for _ in outs],
        compiler_params=pltpu.CompilerParams(vmem_limit_bytes=40 << 20),
        cost_estimate=pl.CostEstimate(
            flops=flops, bytes_accessed=bytes_of(args) + bytes_of(outs), transcendentals=0
        ),
    )(*args)


def exchange(block, distance):
    count = lax.axis_size("leaf")
    return lax.ppermute(block, "leaf", [(i, i ^ distance) for i in range(count)])


def pack_kernel(levels, panel_ref, inverse_ref, update_ref, out_ref):
    rows, panel_rows = inverse_ref.shape[0], update_ref.shape[2]
    out_ref[:rows, :rows] = inverse_ref[...]
    out_ref[rows:, :rows] = jnp.zeros((NOTE_ROWS, rows), bf16)
    for a in range(1, levels):
        columns = pl.ds(rows + (a - 1) * panel_rows, panel_rows)
        out_ref[:rows, columns] = update_ref[a]
        out_ref[rows:, columns] = jnp.full(
            (NOTE_ROWS, panel_rows), panel_ref[0, a].astype(f32)
        ).astype(bf16)


def leaf_up_kernel(
    levels, panel_ref, rhs_ref, inverse_ref, update_ref, sep_rhs_ref, solved_ref, out_ref
):
    k = lax.axis_index("leaf")
    scenarios, sep_rows = sep_rhs_ref.shape
    size, panel_rows = inverse_ref.shape[0], update_ref.shape[2]
    count = sep_rows // panel_rows
    step = min(256, size)
    for low in range(0, size, step):
        high = low + step
        solved_ref[:, low:high] = dot_t(rhs_ref[:, :high], inverse_ref[low:high, :high])
    rounded = solved_ref[...].astype(bf16)
    terms = [dot(rounded, update_ref[a]) for a in range(levels)]
    level = own_level(k, levels)
    wide_level = jnp.minimum(level, levels - 1)
    wide, panel = terms[0], panel_ref[0, 0]
    for a in range(1, levels):
        wide = jnp.where(wide_level == a, terms[a], wide)
        panel = jnp.where(wide_level == a, panel_ref[0, a], panel)
    rhs = jnp.where(level < levels, sep_rhs_ref[...].astype(f32), 0.0)
    out_ref[:scenarios, :sep_rows] = (placed(wide, panel, count) - rhs).astype(bf16)
    out_ref[scenarios:, :sep_rows] = jnp.zeros((NOTE_ROWS, sep_rows), bf16)
    for a in range(levels - 1):
        columns = pl.ds(sep_rows + a * panel_rows, panel_rows)
        later = wide_level <= a
        out_ref[:scenarios, columns] = jnp.where(later, terms[a + 1], terms[a]).astype(bf16)
        panel = jnp.where(later, panel_ref[0, a + 1], panel_ref[0, a])
        out_ref[scenarios:, columns] = jnp.full((NOTE_ROWS, panel_rows), panel.astype(f32)).astype(
            bf16
        )


def hand_on_kernel(step, own_ref, received_ref, factor_ref, carry_ref):
    lower = ((lax.axis_index("leaf") >> step) & 1) == 0
    own, received = own_ref[...], received_ref[...]
    factor_ref[...] = jnp.where(lower, own, received)
    if carry_ref is not None:
        sep_rows = own.shape[0] - NOTE_ROWS
        skipped = own.shape[1] - carry_ref.shape[1]
        following = jnp.where(lower, received, own)
        carry_ref[:, :sep_rows] = following[:, :sep_rows]
        if carry_ref.shape[1] > sep_rows:
            carry_ref[:, sep_rows:] = following[:, sep_rows + skipped :]


def spread_first(message_ref, wide_level, levels, scenarios, sep_rows, panel_rows):
    count = sep_rows // panel_rows
    wide = message_ref[:scenarios, :sep_rows].astype(f32)
    narrow = []
    for a in range(levels - 1):
        columns = pl.ds(sep_rows + a * panel_rows, panel_rows)
        panel = message_ref[scenarios : scenarios + NOTE_ROWS, columns].astype(f32)[:1]
        narrow.append(placed(message_ref[:scenarios, columns].astype(f32), panel, count))
    sums = []
    for a in range(levels):
        value = wide
        if a > 0:
            value = jnp.where(wide_level < a, narrow[a - 1], value)
        if a < levels - 1:
            value = jnp.where(wide_level > a, narrow[a], value)
        sums.append(value)
    return sums


def solve_up(pending, factor_ref, panel_rows):
    scenarios, sep_rows = pending[0].shape
    count = sep_rows // panel_rows
    residual = (-pending[0]).astype(bf16)
    solved = dot_t(residual, factor_ref[:sep_rows, :sep_rows])
    rounded = solved.astype(bf16)
    others = []
    for a, value in enumerate(pending[1:]):
        columns = pl.ds(sep_rows + a * panel_rows, panel_rows)
        panel = factor_ref[sep_rows : sep_rows + NOTE_ROWS, columns].astype(f32)[:1]
        update = dot(rounded, factor_ref[:sep_rows, columns])
        others.append(value + placed(update, panel, count))
    return solved, others


def first_up_kernel(levels, panel_rows, own_ref, received_ref, factor_ref, solved_ref, out_ref):
    k = lax.axis_index("leaf")
    scenarios = own_ref.shape[0] - NOTE_ROWS
    sep_rows = solved_ref.shape[1]
    pending = [
        own + received
        for own, received in zip(
            *(
                spread_first(
                    ref,
                    jnp.minimum(own_level(who, levels), levels - 1),
                    levels,
                    scenarios,
                    sep_rows,
                    panel_rows,
                )
                for ref, who in ((own_ref, k), (received_ref, k ^ 1))
            )
        )
    ]
    solved, others = solve_up(pending, factor_ref, panel_rows)
    solved_ref[...] = solved
    for a, value in enumerate(others):
        out_ref[:, a * sep_rows : (a + 1) * sep_rows] = value.astype(bf16)


def sums_of(own_ref, received_ref, sep_rows):
    return [
        own_ref[:, low : low + sep_rows].astype(f32)
        + received_ref[:, low : low + sep_rows].astype(f32)
        for low in range(0, own_ref.shape[1], sep_rows)
    ]


def up_kernel(panel_rows, own_ref, received_ref, factor_ref, solved_ref, out_ref):
    sep_rows = solved_ref.shape[1]
    pending = sums_of(own_ref, received_ref, sep_rows)
    solved, others = solve_up(pending, factor_ref, panel_rows)
    solved_ref[...] = solved
    for a, value in enumerate(others):
        out_ref[:, a * sep_rows : (a + 1) * sep_rows] = value.astype(bf16)


def down_kernel(levels, *refs):
    panel_ref, own_ref, received_ref, leaf_solved_ref, update_ref, inverse_ref = refs[:6]
    factor_refs = refs[6 : 6 + levels]
    solved_refs = refs[6 + levels : 5 + 2 * levels]
    leaf_out_ref, sep_out_ref, work_ref = refs[5 + 2 * levels :]
    k = lax.axis_index("leaf")
    sep_rows = own_ref.shape[1]
    panel_rows = update_ref.shape[2]
    count = sep_rows // panel_rows
    level = own_level(k, levels)

    top = levels - 1
    pending = sums_of(own_ref, received_ref, sep_rows)
    solved, _ = solve_up(pending, factor_refs[top], panel_rows)
    ancestors = {}
    sep_out = jnp.zeros(sep_out_ref.shape, f32)
    for now in reversed(range(levels)):
        factor_ref = factor_refs[now]
        residual = solved if now == top else solved_refs[now][...]
        for a in range(now + 1, levels):
            columns = pl.ds(sep_rows + (a - now - 1) * panel_rows, panel_rows)
            panel = factor_ref[sep_rows : sep_rows + NOTE_ROWS, columns].astype(f32)[:1]
            block = picked(ancestors[a], panel, count).astype(bf16)
            residual = residual - dot_t(block, factor_ref[:sep_rows, columns])
        solution_now = dot(residual.astype(bf16), factor_ref[:sep_rows, :sep_rows])
        ancestors[now] = solution_now.astype(bf16).astype(f32)
        sep_out = jnp.where(level == now, solution_now, sep_out)
    sep_out_ref[...] = sep_out

    blocks = [picked(ancestors[a], panel_ref[0, a], count).astype(bf16) for a in range(levels)]
    size = inverse_ref.shape[0]
    step = min(256, size)
    for low in range(0, size, step):
        high = low + step
        value = leaf_solved_ref[:, low:high]
        for a in range(levels):
            value = value - dot_t(blocks[a], update_ref[a, low:high, :])
        work_ref[:, low:high] = value.astype(bf16)
    for low in range(0, size, step):
        high = low + step
        leaf_out_ref[:, low:high] = dot(work_ref[:, low:], inverse_ref[low:, low:high])


def local(
    leaf_rhs, sep_rhs, leaf_inverse, leaf_update, leaf_panel, sep_inverse, sep_update, sep_panel
):
    levels = lax.axis_size("leaf").bit_length() - 1
    sep_rows = sep_inverse.shape[0]
    scenarios, size = leaf_rhs.shape
    panel_rows = leaf_update.shape[3]
    tall = sep_rows + NOTE_ROWS
    leaf_update, sep_update = leaf_update[0], sep_update[0]

    (carry,) = call(
        partial(pack_kernel, levels),
        [((tall, sep_rows + (levels - 1) * panel_rows), bf16)],
        (sep_panel, sep_inverse, sep_update),
        smem=(0,),
    )
    arrived = exchange(carry, 1)
    leaf_solved, message = call(
        partial(leaf_up_kernel, levels),
        [
            ((scenarios, size), f32),
            ((scenarios + NOTE_ROWS, sep_rows + (levels - 1) * panel_rows), bf16),
        ],
        (leaf_panel, leaf_rhs, leaf_inverse, leaf_update, sep_rhs),
        smem=(0,),
        flops=2 * scenarios * size * (size + levels * panel_rows),
    )
    factors, solved = [], []
    for now in range(levels):
        received = exchange(message, 1 << now)
        shapes = [(carry.shape, bf16)]
        if now + 1 < levels:
            shapes.append(((tall, sep_rows + (levels - 2 - now) * panel_rows), bf16))
            factor, carry = call(partial(hand_on_kernel, now), shapes, (carry, arrived))
            arrived = exchange(carry, 2 << now)
        else:
            (factor,) = call(
                lambda a, b, c, step=now: hand_on_kernel(step, a, b, c, None),
                shapes,
                (carry, arrived),
            )
        factors.append(factor)
        if now + 1 < levels:
            kernel = (
                partial(first_up_kernel, levels, panel_rows)
                if now == 0
                else partial(up_kernel, panel_rows)
            )
            z, message = call(
                kernel,
                [
                    ((scenarios, sep_rows), f32),
                    ((scenarios, (levels - 1 - now) * sep_rows), bf16),
                ],
                (message, received, factor),
                flops=2 * scenarios * sep_rows * sep_rows * 2,
            )
            solved.append(z)
    args = (leaf_panel, message, received, leaf_solved, leaf_update, leaf_inverse)
    args += tuple(factors) + tuple(solved)
    kernel_args = args
    leaf_out, sep_out = pl.pallas_call(
        partial(down_kernel, levels),
        out_shape=[
            jax.ShapeDtypeStruct((scenarios, size), f32),
            jax.ShapeDtypeStruct((scenarios, sep_rows), f32),
        ],
        in_specs=[pl.BlockSpec(memory_space=pltpu.SMEM)]
        + [pl.BlockSpec(memory_space=pltpu.VMEM)] * (len(kernel_args) - 1),
        out_specs=[pl.BlockSpec(memory_space=pltpu.VMEM)] * 2,
        scratch_shapes=[pltpu.VMEM((scenarios, size), bf16)],
        compiler_params=pltpu.CompilerParams(vmem_limit_bytes=40 << 20),
    )(*kernel_args)
    return leaf_out, sep_out


def solution(mesh):
    return jax.shard_map(
        local,
        mesh=mesh,
        in_specs=(
            P("rhs", "leaf"),
            P("rhs", "leaf"),
            P("leaf", None),
            P("leaf", None, None, None),
            P("leaf", None),
            P("leaf", None),
            P("leaf", None, None, None),
            P("leaf", None),
        ),
        out_specs=(P("rhs", "leaf"), P("rhs", "leaf")),
        check_vma=False,
    )
```

```python
from functools import partial

import jax
import jax.numpy as jnp
from jax import lax
from jax.experimental import pallas as pl
from jax.experimental.pallas import tpu as pltpu
from jax.sharding import PartitionSpec as P

NOTE_ROWS = 16
f32, bf16 = jnp.float32, jnp.bfloat16


def dot(a, b):
    return jnp.dot(a, b, preferred_element_type=f32)


def dot_t(a, b):
    return lax.dot_general(a, b, (((1,), (1,)), ((), ())), preferred_element_type=f32)


def own_level(k, levels):
    level = jnp.int32(0)
    for bit in range(levels):
        low = (2 << bit) - 1
        level = jnp.where((k & low) == low, bit + 1, level)
    return level


def placed(block, panel, count):
    return jnp.concatenate(
        [jnp.where(panel == p, block, jnp.zeros_like(block)) for p in range(count)], axis=1
    )


def picked(vectors, panel, count):
    width = vectors.shape[1] // count
    result = vectors[:, :width]
    for p in range(1, count):
        result = jnp.where(panel == p, vectors[:, p * width : (p + 1) * width], result)
    return result


def call(kernel, outs, args, hbm=(), scratch=(), flops=0):
    def bytes_of(arrays):
        return sum(a.size * a.dtype.itemsize for a in arrays)

    outs = [jax.ShapeDtypeStruct(shape, dtype) for shape, dtype in outs]
    args = [
        pltpu.with_memory_space_constraint(arg, pltpu.HBM) if i in hbm else arg
        for i, arg in enumerate(args)
    ]
    return pl.pallas_call(
        kernel,
        out_shape=outs,
        in_specs=[
            pl.BlockSpec(memory_space=pltpu.HBM if i in hbm else pltpu.VMEM)
            for i in range(len(args))
        ],
        out_specs=[pl.BlockSpec(memory_space=pltpu.VMEM) for _ in outs],
        scratch_shapes=scratch,
        compiler_params=pltpu.CompilerParams(vmem_limit_bytes=40 << 20),
        cost_estimate=pl.CostEstimate(
            flops=flops, bytes_accessed=bytes_of(args) + bytes_of(outs), transcendentals=0
        ),
    )(*args)


def exchange(block, distance):
    count = lax.axis_size("leaf")
    return lax.ppermute(block, "leaf", [(i, i ^ distance) for i in range(count)])


def load_kernel(
    levels,
    panel_hbm,
    sep_inverse_hbm,
    sep_update_hbm,
    leaf_rhs_hbm,
    leaf_inverse_hbm,
    leaf_update_hbm,
    sep_rhs_hbm,
    carry_ref,
    leaf_rhs_ref,
    leaf_inverse_ref,
    leaf_update_ref,
    sep_rhs_ref,
    panel_ref,
    sems,
):
    rows, panel_rows = sep_inverse_hbm.shape[0], sep_update_hbm.shape[2]
    first = [
        (panel_hbm, panel_ref),
        (sep_inverse_hbm, carry_ref.at[pl.ds(0, rows), pl.ds(0, rows)]),
    ]
    for a in range(1, levels):
        columns = pl.ds(rows + (a - 1) * panel_rows, panel_rows)
        first.append((sep_update_hbm.at[a], carry_ref.at[pl.ds(0, rows), columns]))
    second = [(leaf_rhs_hbm, leaf_rhs_ref)]
    size = leaf_inverse_hbm.shape[0]
    step = min(256, size)
    for low in range(0, size, step):
        block = (pl.ds(low, step), pl.ds(0, low + step))
        second.append((leaf_inverse_hbm.at[block], leaf_inverse_ref.at[block]))
    second += [(leaf_update_hbm, leaf_update_ref), (sep_rhs_hbm, sep_rhs_ref)]
    copies = [
        pltpu.make_async_copy(src, dst, sems.at[i]) for i, (src, dst) in enumerate(first + second)
    ]
    for copy in copies:
        copy.start()
    carry_ref[rows:, :rows] = jnp.zeros((NOTE_ROWS, rows), bf16)
    copies[0].wait()
    for a in range(1, levels):
        columns = pl.ds(rows + (a - 1) * panel_rows, panel_rows)
        carry_ref[rows:, columns] = jnp.full(
            (NOTE_ROWS, panel_rows), panel_ref[0, a].astype(f32)
        ).astype(bf16)
    for copy in copies[1:]:
        copy.wait()


def leaf_up_kernel(
    levels,
    panel_hbm,
    rhs_ref,
    inverse_ref,
    update_ref,
    sep_rhs_ref,
    solved_ref,
    own_ref,
    out_ref,
    panel_ref,
    sem,
):
    copy = pltpu.make_async_copy(panel_hbm, panel_ref, sem)
    copy.start()
    k = lax.axis_index("leaf")
    scenarios, sep_rows = sep_rhs_ref.shape
    size, panel_rows = inverse_ref.shape[0], update_ref.shape[2]
    count = sep_rows // panel_rows
    step = min(256, size)
    for low in range(0, size, step):
        high = low + step
        solved_ref[:, low:high] = dot_t(rhs_ref[:, :high], inverse_ref[low:high, :high])
    rounded = solved_ref[...].astype(bf16)
    terms = [dot(rounded, update_ref[a]) for a in range(levels)]
    level = own_level(k, levels)
    wide_level = jnp.minimum(level, levels - 1)
    rhs = jnp.where(level < levels, sep_rhs_ref[...].astype(f32), 0.0)
    copy.wait()
    wide = jnp.zeros((scenarios, sep_rows), f32)
    for a in range(levels):
        spread = placed(terms[a], panel_ref[0, a], count)
        spread = jnp.where(wide_level == a, spread - rhs, spread)
        wide = jnp.where(wide_level == a, spread, wide)
        own_ref[:, a * sep_rows : (a + 1) * sep_rows] = spread
    out_ref[:scenarios, :sep_rows] = wide.astype(bf16)
    out_ref[scenarios:, :sep_rows] = jnp.zeros((NOTE_ROWS, sep_rows), bf16)
    for a in range(levels - 1):
        columns = pl.ds(sep_rows + a * panel_rows, panel_rows)
        later = wide_level <= a
        out_ref[:scenarios, columns] = jnp.where(later, terms[a + 1], terms[a]).astype(bf16)
        panel = jnp.where(later, panel_ref[0, a + 1], panel_ref[0, a])
        out_ref[scenarios:, columns] = jnp.full((NOTE_ROWS, panel_rows), panel.astype(f32)).astype(
            bf16
        )


def hand_on(step, own_ref, received_ref, factor_ref, carry_ref):
    lower = ((lax.axis_index("leaf") >> step) & 1) == 0
    own, received = own_ref[...], received_ref[...]
    factor_ref[...] = jnp.where(lower, own, received)
    if carry_ref is not None:
        sep_rows = own.shape[0] - NOTE_ROWS
        skipped = own.shape[1] - carry_ref.shape[1]
        following = jnp.where(lower, received, own)
        carry_ref[:, :sep_rows] = following[:, :sep_rows]
        if carry_ref.shape[1] > sep_rows:
            carry_ref[:, sep_rows:] = following[:, sep_rows + skipped :]


def spread_first(message_ref, wide_level, levels, scenarios, sep_rows, panel_rows):
    count = sep_rows // panel_rows
    wide = message_ref[:scenarios, :sep_rows].astype(f32)
    narrow = []
    for a in range(levels - 1):
        columns = pl.ds(sep_rows + a * panel_rows, panel_rows)
        panel = message_ref[scenarios : scenarios + NOTE_ROWS, columns].astype(f32)[:1]
        narrow.append(placed(message_ref[:scenarios, columns].astype(f32), panel, count))
    sums = []
    for a in range(levels):
        value = wide
        if a > 0:
            value = jnp.where(wide_level < a, narrow[a - 1], value)
        if a < levels - 1:
            value = jnp.where(wide_level > a, narrow[a], value)
        sums.append(value)
    return sums


def solve_up(pending, factor_ref, panel_rows):
    scenarios, sep_rows = pending[0].shape
    count = sep_rows // panel_rows
    residual = (-pending[0]).astype(bf16)
    solved = dot_t(residual, factor_ref[:sep_rows, :sep_rows])
    rounded = solved.astype(bf16)
    others = []
    for a, value in enumerate(pending[1:]):
        columns = pl.ds(sep_rows + a * panel_rows, panel_rows)
        panel = factor_ref[sep_rows : sep_rows + NOTE_ROWS, columns].astype(f32)[:1]
        update = dot(rounded, factor_ref[:sep_rows, columns])
        others.append(value + placed(update, panel, count))
    return solved, others


def sums_of(own_ref, received, sep_rows):
    return [
        own_ref[:, a * sep_rows : (a + 1) * sep_rows] + value for a, value in enumerate(received)
    ]


def parts_of(ref, sep_rows):
    return [
        ref[:, low : low + sep_rows].astype(f32) for low in range(0, ref.shape[1], sep_rows)
    ]


def up_kernel(
    levels,
    now,
    panel_rows,
    own_ref,
    received_ref,
    factor_ref,
    carry_ref,
    arrived_ref,
    solved_ref,
    sums_ref,
    out_ref,
    next_factor_ref,
    next_carry_ref=None,
):
    scenarios, sep_rows = solved_ref.shape
    hand_on(now + 1, carry_ref, arrived_ref, next_factor_ref, next_carry_ref)
    if now == 0:
        partner = own_level(lax.axis_index("leaf") ^ 1, levels)
        received = spread_first(
            received_ref, jnp.minimum(partner, levels - 1), levels, scenarios, sep_rows, panel_rows
        )
    else:
        received = parts_of(received_ref, sep_rows)
    solved, others = solve_up(sums_of(own_ref, received, sep_rows), factor_ref, panel_rows)
    solved_ref[...] = solved
    for a, value in enumerate(others):
        sums_ref[:, a * sep_rows : (a + 1) * sep_rows] = value
        out_ref[:, a * sep_rows : (a + 1) * sep_rows] = value.astype(bf16)


def down_kernel(levels, *refs):
    panel_hbm, own_ref, received_ref, leaf_solved_ref, update_ref, inverse_ref = refs[:6]
    factor_refs = refs[6 : 6 + levels]
    solved_refs = refs[6 + levels : 5 + 2 * levels]
    leaf_out_ref, sep_out_ref, work_ref, panel_ref, sem = refs[5 + 2 * levels :]
    copy = pltpu.make_async_copy(panel_hbm, panel_ref, sem)
    copy.start()
    k = lax.axis_index("leaf")
    sep_rows = own_ref.shape[1]
    panel_rows = update_ref.shape[2]
    count = sep_rows // panel_rows
    level = own_level(k, levels)

    top = levels - 1
    pending = sums_of(own_ref, parts_of(received_ref, sep_rows), sep_rows)
    solved, _ = solve_up(pending, factor_refs[top], panel_rows)
    ancestors = {}
    sep_out = jnp.zeros(sep_out_ref.shape, f32)
    for now in reversed(range(levels)):
        factor_ref = factor_refs[now]
        residual = solved if now == top else solved_refs[now][...]
        for a in range(now + 1, levels):
            columns = pl.ds(sep_rows + (a - now - 1) * panel_rows, panel_rows)
            panel = factor_ref[sep_rows : sep_rows + NOTE_ROWS, columns].astype(f32)[:1]
            block = picked(ancestors[a], panel, count).astype(bf16)
            residual = residual - dot_t(block, factor_ref[:sep_rows, columns])
        solution_now = dot(residual.astype(bf16), factor_ref[:sep_rows, :sep_rows])
        ancestors[now] = solution_now.astype(bf16).astype(f32)
        sep_out = jnp.where(level == now, solution_now, sep_out)
    sep_out_ref[...] = sep_out

    copy.wait()
    blocks = [picked(ancestors[a], panel_ref[0, a], count).astype(bf16) for a in range(levels)]
    size = inverse_ref.shape[0]
    step = min(256, size)
    for low in range(0, size, step):
        high = low + step
        value = leaf_solved_ref[:, low:high]
        for a in range(levels):
            value = value - dot_t(blocks[a], update_ref[a, low:high, :])
        work_ref[:, low:high] = value.astype(bf16)
    for low in range(0, size, step):
        high = low + step
        leaf_out_ref[:, low:high] = dot(work_ref[:, low:], inverse_ref[low:, low:high])


def local(
    leaf_rhs, sep_rhs, leaf_inverse, leaf_update, leaf_panel, sep_inverse, sep_update, sep_panel
):
    levels = lax.axis_size("leaf").bit_length() - 1
    sep_rows = sep_inverse.shape[0]
    scenarios, size = leaf_rhs.shape
    panel_rows = leaf_update.shape[3]
    tall = sep_rows + NOTE_ROWS
    leaf_update, sep_update = leaf_update[0], sep_update[0]

    panel_smem = pltpu.SMEM(leaf_panel.shape, jnp.int32)
    loaded = call(
        partial(load_kernel, levels),
        [
            ((tall, sep_rows + (levels - 1) * panel_rows), bf16),
            (leaf_rhs.shape, bf16),
            (leaf_inverse.shape, bf16),
            (leaf_update.shape, bf16),
            (sep_rhs.shape, bf16),
        ],
        (sep_panel, sep_inverse, sep_update, leaf_rhs, leaf_inverse, leaf_update, sep_rhs),
        hbm=range(7),
        scratch=[panel_smem, pltpu.SemaphoreType.DMA((levels + 8 + size // 256,))],
    )
    carry, leaf_rhs, leaf_inverse, leaf_update, sep_rhs = loaded
    arrived = exchange(carry, 1)
    leaf_solved, sums, message = call(
        partial(leaf_up_kernel, levels),
        [
            ((scenarios, size), f32),
            ((scenarios, levels * sep_rows), f32),
            ((scenarios + NOTE_ROWS, sep_rows + (levels - 1) * panel_rows), bf16),
        ],
        (leaf_panel, leaf_rhs, leaf_inverse, leaf_update, sep_rhs),
        hbm=(0,),
        scratch=[panel_smem, pltpu.SemaphoreType.DMA],
        flops=2 * scenarios * size * (size + levels * panel_rows),
    )

    def carry_shape(now):
        return ((tall, sep_rows + (levels - 1 - now) * panel_rows), bf16)

    received = exchange(message, 1)
    factor, carry = call(
        partial(hand_on, 0), [carry_shape(0), carry_shape(1)], (carry, arrived)
    )
    factors, solved = [factor], []
    for now in range(levels - 1):
        arrived = exchange(carry, 2 << now)
        shapes = [
            ((scenarios, sep_rows), f32),
            ((scenarios, (levels - 1 - now) * sep_rows), f32),
            ((scenarios, (levels - 1 - now) * sep_rows), bf16),
            carry_shape(now + 1),
        ]
        if now + 2 < levels:
            shapes.append(carry_shape(now + 2))
        results = call(
            partial(up_kernel, levels, now, panel_rows),
            shapes,
            (sums, received, factor, carry, arrived),
            flops=2 * scenarios * sep_rows * sep_rows * 2,
        )
        z, sums, message, factor = results[:4]
        carry = results[4] if now + 2 < levels else None
        solved.append(z)
        factors.append(factor)
        received = exchange(message, 2 << now)
    return call(
        partial(down_kernel, levels),
        [((scenarios, size), f32), ((scenarios, sep_rows), f32)],
        (leaf_panel, sums, received, leaf_solved, leaf_update, leaf_inverse, *factors, *solved),
        hbm=(0,),
        scratch=[pltpu.VMEM((scenarios, size), bf16), panel_smem, pltpu.SemaphoreType.DMA],
        flops=2 * scenarios * size * (size + levels * panel_rows),
    )


def solution(mesh):
    return jax.shard_map(
        local,
        mesh=mesh,
        in_specs=(
            P("rhs", "leaf"),
            P("rhs", "leaf"),
            P("leaf", None),
            P("leaf", None, None, None),
            P("leaf", None),
            P("leaf", None),
            P("leaf", None, None, None),
            P("leaf", None),
        ),
        out_specs=(P("rhs", "leaf"), P("rhs", "leaf")),
        check_vma=False,
    )
```

```python
from functools import partial

import jax
import jax.numpy as jnp
from jax import lax
from jax.experimental import pallas as pl
from jax.experimental.pallas import tpu as pltpu
from jax.sharding import PartitionSpec as P

NOTE_ROWS = 16
GROUPS = 2
f32, bf16 = jnp.float32, jnp.bfloat16


def dot(a, b):
    return jnp.dot(a, b, preferred_element_type=f32)


def dot_t(a, b):
    return lax.dot_general(a, b, (((1,), (1,)), ((), ())), preferred_element_type=f32)


def own_level(k, levels):
    level = jnp.int32(0)
    for bit in range(levels):
        low = (2 << bit) - 1
        level = jnp.where((k & low) == low, bit + 1, level)
    return level


def placed(block, panel, count):
    return jnp.concatenate(
        [jnp.where(panel == p, block, jnp.zeros_like(block)) for p in range(count)], axis=1
    )


def picked(vectors, panel, count):
    width = vectors.shape[1] // count
    result = vectors[:, :width]
    for p in range(1, count):
        result = jnp.where(panel == p, vectors[:, p * width : (p + 1) * width], result)
    return result


def call(kernel, outs, args, hbm=(), hbm_outs=False, aliases=None, scratch=(), flops=0):
    def bytes_of(arrays):
        return sum(a.size * a.dtype.itemsize for a in arrays)

    outs = [jax.ShapeDtypeStruct(shape, dtype) for shape, dtype in outs]
    args = [
        pltpu.with_memory_space_constraint(arg, pltpu.HBM) if i in hbm else arg
        for i, arg in enumerate(args)
    ]
    return pl.pallas_call(
        kernel,
        out_shape=outs,
        in_specs=[
            pl.BlockSpec(memory_space=pltpu.HBM if i in hbm else pltpu.VMEM)
            for i in range(len(args))
        ],
        out_specs=[pl.BlockSpec(memory_space=pltpu.HBM if hbm_outs else pltpu.VMEM) for _ in outs],
        input_output_aliases=aliases or {},
        scratch_shapes=scratch,
        compiler_params=pltpu.CompilerParams(vmem_limit_bytes=40 << 20),
        cost_estimate=pl.CostEstimate(
            flops=flops, bytes_accessed=bytes_of(args) + bytes_of(outs), transcendentals=0
        ),
    )(*args)


def exchange(block, distance, axis="leaf"):
    count = lax.axis_size(axis)
    return lax.ppermute(block, axis, [(i, i ^ distance) for i in range(count)])


def upper_part():
    return lax.axis_index("rhs") & 1


def leaf_up_kernel(
    levels,
    sep_panel_hbm,
    leaf_panel_hbm,
    sep_inverse_hbm,
    sep_update_hbm,
    leaf_rhs_hbm,
    leaf_inverse_hbm,
    leaf_update_hbm,
    sep_rhs_hbm,
    carry_ref,
    leaf_inverse_ref,
    leaf_update_ref,
    solved_ref,
    own_ref,
    *refs,
):
    out_refs = refs[:GROUPS]
    sep_panel_ref, leaf_panel_ref, leaf_rhs_ref, sep_rhs_ref, sems = refs[GROUPS:]
    k = lax.axis_index("leaf")
    scenarios, sep_rows = sep_rhs_hbm.shape
    size, panel_rows = leaf_inverse_hbm.shape[0], leaf_update_hbm.shape[2]
    count = sep_rows // panel_rows
    half = sep_rows // 2
    step = min(256, size)

    started = []

    def bring(source, target):
        copy = pltpu.make_async_copy(source, target, sems.at[len(started)])
        copy.start()
        started.append(copy)
        return copy

    rhs_copy = bring(leaf_rhs_hbm, leaf_rhs_ref)
    inverse_copies = []
    for low in range(0, size, step):
        block = (pl.ds(low, step), pl.ds(0, low + step))
        inverse_copies.append(bring(leaf_inverse_hbm.at[block], leaf_inverse_ref.at[block]))
    update_copy = bring(leaf_update_hbm, leaf_update_ref)
    leaf_panel_copy = bring(leaf_panel_hbm, leaf_panel_ref)
    sep_rhs_copy = bring(sep_rhs_hbm, sep_rhs_ref)
    sep_panel_copy = bring(sep_panel_hbm, sep_panel_ref)
    first_row = pl.multiple_of(upper_part() * half, half)
    factor_copies = [
        bring(
            sep_inverse_hbm.at[pl.ds(first_row, half)],
            carry_ref.at[pl.ds(0, half), pl.ds(0, sep_rows)],
        )
    ]
    for a in range(1, levels):
        columns = pl.ds(sep_rows + (a - 1) * panel_rows, panel_rows)
        factor_copies.append(
            bring(
                sep_update_hbm.at[a, pl.ds(first_row, half)],
                carry_ref.at[pl.ds(0, half), columns],
            )
        )

    rhs_copy.wait()
    rounded = []
    for low, copy in zip(range(0, size, step), inverse_copies):
        high = low + step
        copy.wait()
        value = dot_t(leaf_rhs_ref[:, :high], leaf_inverse_ref[low:high, :high])
        solved_ref[:, low:high] = value
        rounded.append(value.astype(bf16))
    rounded = jnp.concatenate(rounded, axis=1)
    update_copy.wait()
    together = dot(
        rounded, jnp.concatenate([leaf_update_ref[a] for a in range(levels)], axis=1)
    )
    terms = [together[:, a * panel_rows : (a + 1) * panel_rows] for a in range(levels)]

    level = own_level(k, levels)
    wide_level = jnp.minimum(level, levels - 1)
    sep_rhs_copy.wait()
    leaf_panel_copy.wait()
    rhs = jnp.where(level < levels, sep_rhs_ref[...].astype(f32), 0.0)
    wide = jnp.zeros((scenarios, sep_rows), f32)
    for a in range(levels):
        spread = placed(terms[a], leaf_panel_ref[0, a], count)
        spread = jnp.where(wide_level == a, spread - rhs, spread)
        wide = jnp.where(wide_level == a, spread, wide)
        own_ref[:, a * sep_rows : (a + 1) * sep_rows] = spread
    rows = scenarios // GROUPS
    for group, out_ref in enumerate(out_refs):
        low = group * rows
        out_ref[:rows, :sep_rows] = wide[low : low + rows].astype(bf16)
        out_ref[rows:, :sep_rows] = jnp.zeros((NOTE_ROWS, sep_rows), bf16)
        for a in range(levels - 1):
            columns = pl.ds(sep_rows + a * panel_rows, panel_rows)
            later = wide_level <= a
            narrow = jnp.where(later, terms[a + 1], terms[a])
            out_ref[:rows, columns] = narrow[low : low + rows].astype(bf16)
            panel = jnp.where(later, leaf_panel_ref[0, a + 1], leaf_panel_ref[0, a])
            out_ref[rows:, columns] = jnp.full((NOTE_ROWS, panel_rows), panel.astype(f32)).astype(
                bf16
            )

    sep_panel_copy.wait()
    carry_ref[half:, :sep_rows] = jnp.zeros((NOTE_ROWS, sep_rows), bf16)
    for a in range(1, levels):
        columns = pl.ds(sep_rows + (a - 1) * panel_rows, panel_rows)
        carry_ref[half:, columns] = jnp.full(
            (NOTE_ROWS, panel_rows), sep_panel_ref[0, a].astype(f32)
        ).astype(bf16)
    for copy in factor_copies:
        copy.wait()


def hand_on_kernel(step, sep_rows, own_ref, received_ref, factor_ref, carry_ref=None):
    lower = ((lax.axis_index("leaf") >> step) & 1) == 0
    own, received = own_ref[...], received_ref[...]
    factor_ref[...] = jnp.where(lower, own, received)
    if carry_ref is not None:
        skipped = own.shape[1] - carry_ref.shape[1]
        following = jnp.where(lower, received, own)
        carry_ref[:, :sep_rows] = following[:, :sep_rows]
        if carry_ref.shape[1] > sep_rows:
            carry_ref[:, sep_rows:] = following[:, sep_rows + skipped :]


class Factor:
    def __init__(self, own_ref, other_ref, sep_rows, panel_rows):
        self.refs = own_ref, other_ref
        self.sep_rows, self.panel_rows = sep_rows, panel_rows
        self.half = own_ref.shape[0] - NOTE_ROWS

    def columns(self, start, size):
        own, other = (ref[: self.half, start : start + size] for ref in self.refs)
        upper = upper_part() == 1
        return jnp.concatenate([jnp.where(upper, other, own), jnp.where(upper, own, other)], axis=0)

    def inverse(self):
        return self.columns(0, self.sep_rows)

    def updates(self, count):
        return self.columns(self.sep_rows, count * self.panel_rows)

    def panel(self, index):
        start = self.sep_rows + index * self.panel_rows
        notes = self.refs[0][self.half : self.half + NOTE_ROWS, start : start + self.panel_rows]
        return notes.astype(f32)[:1]


def spread_first(message_ref, wide_level, levels, rows, sep_rows, panel_rows):
    count = sep_rows // panel_rows
    wide = message_ref[:rows, :sep_rows].astype(f32)
    narrow = []
    for a in range(levels - 1):
        columns = pl.ds(sep_rows + a * panel_rows, panel_rows)
        panel = message_ref[rows : rows + NOTE_ROWS, columns].astype(f32)[:1]
        narrow.append(placed(message_ref[:rows, columns].astype(f32), panel, count))
    sums = []
    for a in range(levels):
        value = wide
        if a > 0:
            value = jnp.where(wide_level < a, narrow[a - 1], value)
        if a < levels - 1:
            value = jnp.where(wide_level > a, narrow[a], value)
        sums.append(value)
    return sums


def solve_up(pending, factor):
    count = factor.sep_rows // factor.panel_rows
    solved = dot_t((-pending[0]).astype(bf16), factor.inverse())
    others = []
    if len(pending) > 1:
        updates = dot(solved.astype(bf16), factor.updates(len(pending) - 1))
        for a, value in enumerate(pending[1:]):
            update = updates[:, a * factor.panel_rows : (a + 1) * factor.panel_rows]
            others.append(value + placed(update, factor.panel(a), count))
    return solved, others


def sums_of(own_ref, first, received):
    rows, sep_rows = received[0].shape
    return [
        own_ref[first : first + rows, a * sep_rows : (a + 1) * sep_rows] + value
        for a, value in enumerate(received)
    ]


def parts_of(ref, sep_rows):
    return [ref[:, low : low + sep_rows].astype(f32) for low in range(0, ref.shape[1], sep_rows)]


def up_kernel(
    levels,
    now,
    first,
    panel_rows,
    own_ref,
    received_ref,
    factor_ref,
    other_ref,
    solved_ref,
    sums_ref,
    out_ref,
):
    rows, sep_rows = solved_ref.shape
    if now == 0:
        partner = jnp.minimum(own_level(lax.axis_index("leaf") ^ 1, levels), levels - 1)
        received = spread_first(received_ref, partner, levels, rows, sep_rows, panel_rows)
    else:
        received = parts_of(received_ref, sep_rows)
    factor = Factor(factor_ref, other_ref, sep_rows, panel_rows)
    solved, others = solve_up(sums_of(own_ref, first, received), factor)
    solved_ref[...] = solved
    for a, value in enumerate(others):
        sums_ref[:, a * sep_rows : (a + 1) * sep_rows] = value
        out_ref[:, a * sep_rows : (a + 1) * sep_rows] = value.astype(bf16)


def down_kernel(levels, first, earlier, *refs):
    panel_hbm, own_ref, received_ref, leaf_solved_ref, update_ref, inverse_ref = refs[:6]
    factor_refs = refs[6 : 6 + 2 * levels]
    solved_refs = refs[6 + 2 * levels : 5 + 3 * levels]
    refs = refs[5 + 3 * levels + (2 if earlier else 0) :]
    leaf_out_hbm, sep_out_hbm, work_ref, leaf_out_ref, sep_out_ref, panel_ref, sems = refs
    copy = pltpu.make_async_copy(panel_hbm, panel_ref, sems.at[0])
    copy.start()
    k = lax.axis_index("leaf")
    rows, sep_rows = own_ref.shape
    panel_rows = update_ref.shape[2]
    count = sep_rows // panel_rows
    level = own_level(k, levels)
    factors = [
        Factor(factor_refs[2 * now], factor_refs[2 * now + 1], sep_rows, panel_rows)
        for now in range(levels)
    ]

    top = levels - 1
    pending = sums_of(own_ref, 0, parts_of(received_ref, sep_rows))
    solved, _ = solve_up(pending, factors[top])
    ancestors = {}
    sep_out = jnp.zeros((rows, sep_rows), f32)
    for now in reversed(range(levels)):
        factor = factors[now]
        residual = solved
        if now < top:
            blocks = [
                picked(ancestors[a], factor.panel(a - now - 1), count).astype(bf16)
                for a in range(now + 1, levels)
            ]
            residual = solved_refs[now][...] - dot_t(
                jnp.concatenate(blocks, axis=1), factor.updates(top - now)
            )
        solution_now = dot(residual.astype(bf16), factor.inverse())
        ancestors[now] = solution_now.astype(bf16).astype(f32)
        sep_out = jnp.where(level == now, solution_now, sep_out)
    sep_out_ref[...] = sep_out
    here = pl.ds(first, rows)
    leaving = [pltpu.make_async_copy(sep_out_ref, sep_out_hbm.at[here], sems.at[1])]
    leaving[0].start()

    copy.wait()
    blocks = jnp.concatenate(
        [picked(ancestors[a], panel_ref[0, a], count).astype(bf16) for a in range(levels)], axis=1
    )
    size = inverse_ref.shape[0]
    step = min(256, size)
    for low in range(0, size, step):
        high = low + step
        updates = jnp.concatenate([update_ref[a, low:high, :] for a in range(levels)], axis=1)
        value = leaf_solved_ref[first : first + rows, low:high] - dot_t(blocks, updates)
        work_ref[:, low:high] = value.astype(bf16)
    for low in range(0, size, step):
        high = low + step
        leaf_out_ref[:, low:high] = dot(work_ref[:, low:], inverse_ref[low:, low:high])
        columns = pl.ds(low, step)
        leaving.append(
            pltpu.make_async_copy(
                leaf_out_ref.at[:, columns],
                leaf_out_hbm.at[here, columns],
                sems.at[len(leaving) + 1],
            )
        )
        leaving[-1].start()
    for copy in leaving:
        copy.wait()


def local(
    leaf_rhs, sep_rhs, leaf_inverse, leaf_update, leaf_panel, sep_inverse, sep_update, sep_panel
):
    levels = lax.axis_size("leaf").bit_length() - 1
    sep_rows = sep_inverse.shape[0]
    scenarios, size = leaf_rhs.shape
    panel_rows = leaf_update.shape[3]
    rows = scenarios // GROUPS
    panel_smem = pltpu.SMEM(leaf_panel.shape, jnp.int32)
    sems = pltpu.SemaphoreType.DMA((levels + 8 + size // min(256, size),))

    def carry_shape(now):
        width = sep_rows + (levels - 1 - now) * panel_rows
        return ((sep_rows // 2 + NOTE_ROWS, width), bf16)

    results = call(
        partial(leaf_up_kernel, levels),
        [
            carry_shape(0),
            (leaf_inverse.shape, bf16),
            (leaf_update.shape[1:], bf16),
            ((scenarios, size), f32),
            ((scenarios, levels * sep_rows), f32),
        ]
        + [((rows + NOTE_ROWS, sep_rows + (levels - 1) * panel_rows), bf16)] * GROUPS,
        (
            sep_panel,
            leaf_panel,
            sep_inverse,
            sep_update[0],
            leaf_rhs,
            leaf_inverse,
            leaf_update[0],
            sep_rhs,
        ),
        hbm=range(8),
        scratch=[
            panel_smem,
            panel_smem,
            pltpu.VMEM(leaf_rhs.shape, bf16),
            pltpu.VMEM(sep_rhs.shape, bf16),
            sems,
        ],
        flops=2 * scenarios * size * (size + levels * panel_rows),
    )
    carry, leaf_inverse, leaf_update, leaf_solved, own = results[:5]
    sums, messages = [own] * GROUPS, results[5:]
    arrived = exchange(carry, 1)
    received = [exchange(message, 1) for message in messages]
    factors, solved = [], [[] for _ in range(GROUPS)]
    for now in range(levels):
        shapes = [carry_shape(now)]
        if now + 1 < levels:
            shapes.append(carry_shape(now + 1))
        handed = call(partial(hand_on_kernel, now, sep_rows), shapes, (carry, arrived))
        factors += [handed[0], exchange(handed[0], 1, "rhs")]
        if now + 1 == levels:
            break
        carry = handed[1]
        arrived = exchange(carry, 2 << now)
        for group in range(GROUPS):
            z, sums[group], message = call(
                partial(up_kernel, levels, now, group * rows if now == 0 else 0, panel_rows),
                [
                    ((rows, sep_rows), f32),
                    ((rows, (levels - 1 - now) * sep_rows), f32),
                    ((rows, (levels - 1 - now) * sep_rows), bf16),
                ],
                (sums[group], received[group], *factors[-2:]),
                flops=2 * rows * sep_rows * sep_rows * 2,
            )
            solved[group].append(z)
            received[group] = exchange(message, 2 << now)
    outputs = []
    for group in range(GROUPS):
        args = (leaf_panel, sums[group], received[group], leaf_solved, leaf_update, leaf_inverse)
        args += (*factors, *solved[group])
        count = len(args)
        outputs = call(
            partial(down_kernel, levels, group * rows, group > 0),
            [((scenarios, size), f32), ((scenarios, sep_rows), f32)],
            args + tuple(outputs),
            hbm=(0, count, count + 1),
            hbm_outs=True,
            aliases={count: 0, count + 1: 1} if group else None,
            scratch=[
                pltpu.VMEM((rows, size), bf16),
                pltpu.VMEM((rows, size), f32),
                pltpu.VMEM((rows, sep_rows), f32),
                panel_smem,
                sems,
            ],
            flops=2 * rows * size * (size + levels * panel_rows),
        )
    return tuple(outputs)


def solution(mesh):
    return jax.shard_map(
        local,
        mesh=mesh,
        in_specs=(
            P("rhs", "leaf"),
            P("rhs", "leaf"),
            P("leaf", None),
            P("leaf", None, None, None),
            P("leaf", None),
            P("leaf", None),
            P("leaf", None, None, None),
            P("leaf", None),
        ),
        out_specs=(P("rhs", "leaf"), P("rhs", "leaf")),
        check_vma=False,
    )
```

```python
from functools import partial

import jax
import jax.numpy as jnp
from jax import lax
from jax.experimental import pallas as pl
from jax.experimental.pallas import tpu as pltpu
from jax.sharding import PartitionSpec as P

NOTE_ROWS = 16
f32, bf16 = jnp.float32, jnp.bfloat16


def dot(a, b):
    return jnp.dot(a, b, preferred_element_type=f32)


def dot_t(a, b):
    return lax.dot_general(a, b, (((1,), (1,)), ((), ())), preferred_element_type=f32)


def own_level(k, levels):
    level = jnp.int32(0)
    for bit in range(levels):
        low = (2 << bit) - 1
        level = jnp.where((k & low) == low, bit + 1, level)
    return level


def placed(block, panel, count):
    return jnp.concatenate(
        [jnp.where(panel == p, block, jnp.zeros_like(block)) for p in range(count)], axis=1
    )


def picked(vectors, panel, count):
    width = vectors.shape[1] // count
    result = vectors[:, :width]
    for p in range(1, count):
        result = jnp.where(panel == p, vectors[:, p * width : (p + 1) * width], result)
    return result


def call(kernel, outs, args, hbm=(), hbm_outs=False, scratch=(), flops=0):
    def bytes_of(arrays):
        return sum(a.size * a.dtype.itemsize for a in arrays)

    outs = [jax.ShapeDtypeStruct(shape, dtype) for shape, dtype in outs]
    args = [
        pltpu.with_memory_space_constraint(arg, pltpu.HBM) if i in hbm else arg
        for i, arg in enumerate(args)
    ]
    return pl.pallas_call(
        kernel,
        out_shape=outs,
        in_specs=[
            pl.BlockSpec(memory_space=pltpu.HBM if i in hbm else pltpu.VMEM)
            for i in range(len(args))
        ],
        out_specs=[pl.BlockSpec(memory_space=pltpu.HBM if hbm_outs else pltpu.VMEM) for _ in outs],
        scratch_shapes=scratch,
        compiler_params=pltpu.CompilerParams(vmem_limit_bytes=40 << 20),
        cost_estimate=pl.CostEstimate(
            flops=flops, bytes_accessed=bytes_of(args) + bytes_of(outs), transcendentals=0
        ),
    )(*args)


def exchange(block, distance, axis="leaf", upward=False):
    route = [(i, i ^ distance) for i in range(lax.axis_size(axis))]
    return lax.ppermute(block, axis, [pair for pair in route if not upward or pair[0] < pair[1]])


def upper_part():
    return lax.axis_index("rhs") & 1


def load_kernel(
    levels,
    sep_panel_hbm,
    leaf_panel_hbm,
    sep_inverse_hbm,
    sep_update_hbm,
    leaf_rhs_hbm,
    leaf_inverse_hbm,
    leaf_update_hbm,
    sep_rhs_hbm,
    carry_ref,
    leaf_rhs_ref,
    leaf_inverse_ref,
    leaf_update_ref,
    sep_rhs_ref,
    sep_panel_ref,
    leaf_panel_ref,
    sems,
):
    sep_rows = sep_rhs_hbm.shape[1]
    size, panel_rows = leaf_inverse_hbm.shape[0], leaf_update_hbm.shape[2]
    half = sep_rows // 2
    step = min(256, size)
    copies = []

    def bring(source, target):
        copies.append(pltpu.make_async_copy(source, target, sems.at[len(copies)]))
        copies[-1].start()

    bring(sep_panel_hbm, sep_panel_ref)
    bring(leaf_panel_hbm, leaf_panel_ref)
    rows = pl.ds(pl.multiple_of(upper_part() * half, half), half)
    bring(sep_inverse_hbm.at[rows], carry_ref.at[pl.ds(0, half), pl.ds(0, sep_rows)])
    for a in range(1, levels):
        columns = pl.ds(sep_rows + (a - 1) * panel_rows, panel_rows)
        bring(sep_update_hbm.at[a, rows], carry_ref.at[pl.ds(0, half), columns])
    bring(leaf_rhs_hbm, leaf_rhs_ref)
    for low in range(0, size, step):
        block = (pl.ds(low, step), pl.ds(0, low + step))
        bring(leaf_inverse_hbm.at[block], leaf_inverse_ref.at[block])
    bring(leaf_update_hbm, leaf_update_ref)
    bring(sep_rhs_hbm, sep_rhs_ref)

    copies[0].wait()
    copies[1].wait()
    row = lax.broadcasted_iota(jnp.int32, (NOTE_ROWS, sep_rows), 0)
    notes = jnp.zeros((NOTE_ROWS, sep_rows), f32)
    for a in range(levels):
        notes = jnp.where(row == a, leaf_panel_ref[0, a].astype(f32), notes)
    carry_ref[half:, :sep_rows] = notes.astype(bf16)
    for a in range(1, levels):
        columns = pl.ds(sep_rows + (a - 1) * panel_rows, panel_rows)
        carry_ref[half:, columns] = jnp.full(
            (NOTE_ROWS, panel_rows), sep_panel_ref[0, a].astype(f32)
        ).astype(bf16)
    for copy in copies[2:]:
        copy.wait()


def leaf_up_kernel(
    levels, carry_ref, rhs_ref, inverse_ref, update_ref, sep_rhs_ref, solved_ref, own_ref, out_ref
):
    k = lax.axis_index("leaf")
    scenarios, sep_rows = sep_rhs_ref.shape
    size, panel_rows = inverse_ref.shape[0], update_ref.shape[2]
    count = sep_rows // panel_rows
    step = min(256, size)
    rounded = []
    for low in range(0, size, step):
        high = low + step
        value = dot_t(rhs_ref[:, :high], inverse_ref[low:high, :high])
        solved_ref[:, low:high] = value
        rounded.append(value.astype(bf16))
    updates = jnp.concatenate([update_ref[a] for a in range(levels)], axis=1)
    together = dot(jnp.concatenate(rounded, axis=1), updates)
    terms = [together[:, a * panel_rows : (a + 1) * panel_rows] for a in range(levels)]
    level = own_level(k, levels)
    wide_level = jnp.minimum(level, levels - 1)
    rhs = jnp.where(level < levels, sep_rhs_ref[...].astype(f32), 0.0)
    wide = jnp.zeros((scenarios, sep_rows), f32)
    for a in range(levels):
        spread = placed(terms[a], leaf_panel(carry_ref, a, panel_rows), count)
        spread = jnp.where(wide_level == a, spread - rhs, spread)
        wide = jnp.where(wide_level == a, spread, wide)
        own_ref[:, a * sep_rows : (a + 1) * sep_rows] = spread
    out_ref[:, :sep_rows] = wide.astype(bf16)
    for a in range(levels - 1):
        columns = pl.ds(sep_rows + a * panel_rows, panel_rows)
        out_ref[:, columns] = jnp.where(wide_level <= a, terms[a + 1], terms[a]).astype(bf16)


def leaf_panel(first_carry_ref, level, panel_rows):
    rows = first_carry_ref.shape[0]
    notes = first_carry_ref[rows - NOTE_ROWS :, :panel_rows].astype(f32)
    return notes[level : level + 1]


def hand_on_kernel(step, sep_rows, own_ref, received_ref, factor_ref, carry_ref=None):
    lower = ((lax.axis_index("leaf") >> step) & 1) == 0
    own, received = own_ref[...], received_ref[...]
    factor_ref[...] = jnp.where(lower, own, received)
    if carry_ref is not None:
        skipped = own.shape[1] - carry_ref.shape[1]
        following = jnp.where(lower, received, own)
        carry_ref[:, :sep_rows] = following[:, :sep_rows]
        if carry_ref.shape[1] > sep_rows:
            carry_ref[:, sep_rows:] = following[:, sep_rows + skipped :]


class Factor:
    def __init__(self, own_ref, other_ref, sep_rows, panel_rows):
        self.refs = own_ref, other_ref
        self.sep_rows, self.panel_rows = sep_rows, panel_rows
        self.half = own_ref.shape[0] - NOTE_ROWS

    def columns(self, start, size):
        own, other = (ref[: self.half, start : start + size] for ref in self.refs)
        upper = upper_part() == 1
        return jnp.concatenate([jnp.where(upper, other, own), jnp.where(upper, own, other)], axis=0)

    def inverse(self):
        return self.columns(0, self.sep_rows)

    def updates(self, count):
        return self.columns(self.sep_rows, count * self.panel_rows)

    def panel(self, index):
        start = self.sep_rows + index * self.panel_rows
        notes = self.refs[0][self.half : self.half + NOTE_ROWS, start : start + self.panel_rows]
        return notes.astype(f32)[:1]


def spread_first(message_ref, arrived_ref, wide_level, levels, sep_rows, panel_rows):
    count = sep_rows // panel_rows
    wide = message_ref[:, :sep_rows].astype(f32)
    sums = []
    for level in range(levels):
        value = wide
        panel = leaf_panel(arrived_ref, level, panel_rows)
        for a, here in ((level - 1, wide_level < level), (level, wide_level > level)):
            if 0 <= a < levels - 1:
                columns = pl.ds(sep_rows + a * panel_rows, panel_rows)
                narrow = placed(message_ref[:, columns].astype(f32), panel, count)
                value = jnp.where(here, narrow, value)
        sums.append(value)
    return sums


def solve_up(pending, factor):
    count = factor.sep_rows // factor.panel_rows
    solved = dot_t((-pending[0]).astype(bf16), factor.inverse())
    others = []
    if len(pending) > 1:
        updates = dot(solved.astype(bf16), factor.updates(len(pending) - 1))
        for a, value in enumerate(pending[1:]):
            update = updates[:, a * factor.panel_rows : (a + 1) * factor.panel_rows]
            others.append(value + placed(update, factor.panel(a), count))
    return solved, others


def sums_of(own_ref, received):
    sep_rows = received[0].shape[1]
    return [
        own_ref[:, a * sep_rows : (a + 1) * sep_rows] + value for a, value in enumerate(received)
    ]


def parts_of(ref, sep_rows):
    return [ref[:, low : low + sep_rows].astype(f32) for low in range(0, ref.shape[1], sep_rows)]


def up_kernel(
    levels, now, panel_rows, own_ref, received_ref, factor_ref, other_ref, arrived_ref, *refs
):
    solved_ref, sums_ref, out_ref = refs[-3:]
    sep_rows = solved_ref.shape[1]
    if now == 0:
        partner = jnp.minimum(own_level(lax.axis_index("leaf") ^ 1, levels), levels - 1)
        received = spread_first(received_ref, arrived_ref, partner, levels, sep_rows, panel_rows)
    else:
        received = parts_of(received_ref, sep_rows)
    factor = Factor(factor_ref, other_ref, sep_rows, panel_rows)
    solved, others = solve_up(sums_of(own_ref, received), factor)
    solved_ref[...] = solved
    for a, value in enumerate(others):
        sums_ref[:, a * sep_rows : (a + 1) * sep_rows] = value
        out_ref[:, a * sep_rows : (a + 1) * sep_rows] = value.astype(bf16)


def down_kernel(levels, *refs):
    panel_hbm, own_ref, received_ref, leaf_solved_ref, update_ref, inverse_ref = refs[:6]
    factor_refs = refs[6 : 6 + 2 * levels]
    solved_refs = refs[6 + 2 * levels : 5 + 3 * levels]
    leaf_out_hbm, sep_out_hbm, work_ref, leaf_out_ref, sep_out_ref, panel_ref, sems = refs[
        5 + 3 * levels :
    ]
    copy = pltpu.make_async_copy(panel_hbm, panel_ref, sems.at[0])
    copy.start()
    k = lax.axis_index("leaf")
    rows, sep_rows = own_ref.shape
    panel_rows = update_ref.shape[2]
    count = sep_rows // panel_rows
    level = own_level(k, levels)
    factors = [
        Factor(factor_refs[2 * now], factor_refs[2 * now + 1], sep_rows, panel_rows)
        for now in range(levels)
    ]

    top = levels - 1
    pending = sums_of(own_ref, parts_of(received_ref, sep_rows))
    solved, _ = solve_up(pending, factors[top])
    ancestors = {}
    sep_out = jnp.zeros((rows, sep_rows), f32)
    for now in reversed(range(levels)):
        factor = factors[now]
        residual = solved
        if now < top:
            blocks = [
                picked(ancestors[a], factor.panel(a - now - 1), count).astype(bf16)
                for a in range(now + 1, levels)
            ]
            residual = solved_refs[now][...] - dot_t(
                jnp.concatenate(blocks, axis=1), factor.updates(top - now)
            )
        solution_now = dot(residual.astype(bf16), factor.inverse())
        ancestors[now] = solution_now.astype(bf16).astype(f32)
        sep_out = jnp.where(level == now, solution_now, sep_out)
    sep_out_ref[...] = sep_out
    leaving = [pltpu.make_async_copy(sep_out_ref, sep_out_hbm, sems.at[1])]
    leaving[0].start()

    copy.wait()
    blocks = jnp.concatenate(
        [picked(ancestors[a], panel_ref[0, a], count).astype(bf16) for a in range(levels)], axis=1
    )
    size = inverse_ref.shape[0]
    step = min(256, size)
    for low in range(0, size, step):
        high = low + step
        updates = jnp.concatenate([update_ref[a, low:high, :] for a in range(levels)], axis=1)
        value = leaf_solved_ref[:, low:high] - dot_t(blocks, updates)
        work_ref[:, low:high] = value.astype(bf16)
    for low in range(0, size, step):
        high = low + step
        leaf_out_ref[:, low:high] = dot(work_ref[:, low:], inverse_ref[low:, low:high])
        columns = pl.ds(low, step)
        leaving.append(
            pltpu.make_async_copy(
                leaf_out_ref.at[:, columns],
                leaf_out_hbm.at[:, columns],
                sems.at[len(leaving) + 1],
            )
        )
        leaving[-1].start()
    for copy in leaving:
        copy.wait()


def local(
    leaf_rhs, sep_rhs, leaf_inverse, leaf_update, leaf_panel, sep_inverse, sep_update, sep_panel
):
    levels = lax.axis_size("leaf").bit_length() - 1
    sep_rows = sep_inverse.shape[0]
    scenarios, size = leaf_rhs.shape
    leaf_update, sep_update = leaf_update[0], sep_update[0]
    panel_rows = leaf_update.shape[2]
    panel_smem = pltpu.SMEM(leaf_panel.shape, jnp.int32)
    sems = pltpu.SemaphoreType.DMA((levels + 8 + size // min(256, size),))
    leaf_flops = 2 * scenarios * size * (size + levels * panel_rows)

    def carry_shape(now):
        width = sep_rows + (levels - 1 - now) * panel_rows
        return ((sep_rows // 2 + NOTE_ROWS, width), bf16)

    loaded = (leaf_rhs, leaf_inverse, leaf_update, sep_rhs)
    carry, *loaded = call(
        partial(load_kernel, levels),
        [carry_shape(0)] + [(array.shape, bf16) for array in loaded],
        (sep_panel, leaf_panel, sep_inverse, sep_update, *loaded),
        hbm=range(8),
        scratch=[panel_smem, panel_smem, sems],
    )
    arrived = exchange(carry, 1)
    leaf_solved, sums, message = call(
        partial(leaf_up_kernel, levels),
        [
            ((scenarios, size), f32),
            ((scenarios, levels * sep_rows), f32),
            ((scenarios, sep_rows + (levels - 1) * panel_rows), bf16),
        ],
        (carry, *loaded),
        flops=leaf_flops,
    )
    received = exchange(message, 1)
    first_arrived = arrived
    factors, solved = [], []
    for now in range(levels):
        shapes = [carry_shape(now)]
        if now + 1 < levels:
            shapes.append(carry_shape(now + 1))
        handed = call(partial(hand_on_kernel, now, sep_rows), shapes, (carry, arrived))
        factors += [handed[0], exchange(handed[0], 1, "rhs")]
        if now + 1 == levels:
            break
        carry = handed[1]
        arrived = exchange(carry, 2 << now, upward=now + 2 == levels)
        z, sums, message = call(
            partial(up_kernel, levels, now, panel_rows),
            [
                ((scenarios, sep_rows), f32),
                ((scenarios, (levels - 1 - now) * sep_rows), f32),
                ((scenarios, (levels - 1 - now) * sep_rows), bf16),
            ],
            (sums, received, *factors[-2:], first_arrived, arrived)[: 6 if now + 2 < levels else 5],
            flops=2 * scenarios * sep_rows * sep_rows * 2,
        )
        solved.append(z)
        received = exchange(message, 2 << now)
    _, leaf_inverse, leaf_update, _ = loaded
    return call(
        partial(down_kernel, levels),
        [((scenarios, size), f32), ((scenarios, sep_rows), f32)],
        (leaf_panel, sums, received, leaf_solved, leaf_update, leaf_inverse, *factors, *solved),
        hbm=(0,),
        hbm_outs=True,
        scratch=[
            pltpu.VMEM((scenarios, size), bf16),
            pltpu.VMEM((scenarios, size), f32),
            pltpu.VMEM((scenarios, sep_rows), f32),
            panel_smem,
            sems,
        ],
        flops=leaf_flops,
    )


def solution(mesh):
    return jax.shard_map(
        local,
        mesh=mesh,
        in_specs=(
            P("rhs", "leaf"),
            P("rhs", "leaf"),
            P("leaf", None),
            P("leaf", None, None, None),
            P("leaf", None),
            P("leaf", None),
            P("leaf", None, None, None),
            P("leaf", None),
        ),
        out_specs=(P("rhs", "leaf"), P("rhs", "leaf")),
        check_vma=False,
    )
```

```python
from functools import partial

import jax
import jax.numpy as jnp
from jax import lax
from jax.experimental import pallas as pl
from jax.experimental.pallas import tpu as pltpu
from jax.sharding import PartitionSpec as P

NOTE_ROWS = 16
f32, bf16 = jnp.float32, jnp.bfloat16


def dot(a, b):
    return jnp.dot(a, b, preferred_element_type=f32)


def dot_t(a, b):
    return lax.dot_general(a, b, (((1,), (1,)), ((), ())), preferred_element_type=f32)


def own_level(k, levels):
    level = jnp.int32(0)
    for bit in range(levels):
        low = (2 << bit) - 1
        level = jnp.where((k & low) == low, bit + 1, level)
    return level


def placed(block, panel, count):
    return jnp.concatenate(
        [jnp.where(panel == p, block, jnp.zeros_like(block)) for p in range(count)], axis=1
    )


def picked(vectors, panel, count):
    width = vectors.shape[1] // count
    result = vectors[:, :width]
    for p in range(1, count):
        result = jnp.where(panel == p, vectors[:, p * width : (p + 1) * width], result)
    return result


def call(kernel, outs, args, hbm=(), hbm_outs=False, scratch=(), flops=0):
    def bytes_of(arrays):
        return sum(a.size * a.dtype.itemsize for a in arrays)

    outs = [jax.ShapeDtypeStruct(shape, dtype) for shape, dtype in outs]
    args = [
        pltpu.with_memory_space_constraint(arg, pltpu.HBM) if i in hbm else arg
        for i, arg in enumerate(args)
    ]
    return pl.pallas_call(
        kernel,
        out_shape=outs,
        in_specs=[
            pl.BlockSpec(memory_space=pltpu.HBM if i in hbm else pltpu.VMEM)
            for i in range(len(args))
        ],
        out_specs=[pl.BlockSpec(memory_space=pltpu.HBM if hbm_outs else pltpu.VMEM) for _ in outs],
        scratch_shapes=scratch,
        compiler_params=pltpu.CompilerParams(vmem_limit_bytes=40 << 20),
        cost_estimate=pl.CostEstimate(
            flops=flops, bytes_accessed=bytes_of(args) + bytes_of(outs), transcendentals=0
        ),
    )(*args)


def exchange(block, distance, axis="leaf", upward=False):
    route = [(i, i ^ distance) for i in range(lax.axis_size(axis))]
    return lax.ppermute(block, axis, [pair for pair in route if not upward or pair[0] < pair[1]])


def upper_part():
    return lax.axis_index("rhs") & 1


def pack_kernel(
    levels,
    sep_panel_hbm,
    leaf_panel_hbm,
    sep_inverse_hbm,
    sep_update_hbm,
    carry_ref,
    sep_panel_ref,
    leaf_panel_ref,
    sems,
):
    sep_rows, panel_rows = sep_inverse_hbm.shape[1], sep_update_hbm.shape[2]
    half = sep_rows // 2
    copies = []

    def bring(source, target):
        copies.append(pltpu.make_async_copy(source, target, sems.at[len(copies)]))
        copies[-1].start()

    bring(sep_panel_hbm, sep_panel_ref)
    bring(leaf_panel_hbm, leaf_panel_ref)
    rows = pl.ds(pl.multiple_of(upper_part() * half, half), half)
    bring(sep_inverse_hbm.at[rows], carry_ref.at[pl.ds(0, half), pl.ds(0, sep_rows)])
    for a in range(1, levels):
        columns = pl.ds(sep_rows + (a - 1) * panel_rows, panel_rows)
        bring(sep_update_hbm.at[a, rows], carry_ref.at[pl.ds(0, half), columns])

    copies[0].wait()
    copies[1].wait()
    row = lax.broadcasted_iota(jnp.int32, (NOTE_ROWS, sep_rows), 0)
    notes = jnp.zeros((NOTE_ROWS, sep_rows), f32)
    for a in range(levels):
        notes = jnp.where(row == a, leaf_panel_ref[0, a].astype(f32), notes)
    carry_ref[half:, :sep_rows] = notes.astype(bf16)
    for a in range(1, levels):
        columns = pl.ds(sep_rows + (a - 1) * panel_rows, panel_rows)
        carry_ref[half:, columns] = jnp.full(
            (NOTE_ROWS, panel_rows), sep_panel_ref[0, a].astype(f32)
        ).astype(bf16)
    for copy in copies[2:]:
        copy.wait()


def leaf_up_kernel(
    levels,
    carry_ref,
    rhs_hbm,
    inverse_hbm,
    update_hbm,
    sep_rhs_hbm,
    inverse_ref,
    update_ref,
    solved_ref,
    own_ref,
    out_ref,
    rhs_ref,
    sep_rhs_ref,
    sems,
):
    k = lax.axis_index("leaf")
    sep_rows = sep_rhs_ref.shape[1]
    size, panel_rows = inverse_ref.shape[0], update_ref.shape[2]
    count = sep_rows // panel_rows
    step = min(256, size)
    lows = range(0, size, step)
    copies = []

    def bring(source, target):
        copies.append(pltpu.make_async_copy(source, target, sems.at[len(copies)]))
        copies[-1].start()

    bring(rhs_hbm, rhs_ref)
    for low in lows:
        block = (pl.ds(low, step), pl.ds(0, low + step))
        bring(inverse_hbm.at[block], inverse_ref.at[block])
    bring(update_hbm, update_ref)
    bring(sep_rhs_hbm, sep_rhs_ref)

    def solve(low):
        high = low + step
        value = dot_t(rhs_ref[:, :high], inverse_ref[low:high, :high])
        solved_ref[:, low:high] = value
        return value.astype(bf16)

    early = len(copies) - 3
    for copy in copies[:early]:
        copy.wait()
    rounded = [solve(low) for low in lows[:-1]]
    for copy in copies[early:]:
        copy.wait()
    rounded.append(solve(lows[-1]))
    updates = jnp.concatenate([update_ref[a] for a in range(levels)], axis=1)
    together = dot(jnp.concatenate(rounded, axis=1), updates)
    terms = [together[:, a * panel_rows : (a + 1) * panel_rows] for a in range(levels)]
    level = own_level(k, levels)
    wide_level = jnp.minimum(level, levels - 1)
    rhs = jnp.where(level < levels, sep_rhs_ref[...].astype(f32), 0.0)
    wide = jnp.zeros(rhs.shape, f32)
    for a in range(levels):
        spread = placed(terms[a], leaf_panel(carry_ref, a, panel_rows), count)
        spread = jnp.where(wide_level == a, spread - rhs, spread)
        wide = jnp.where(wide_level == a, spread, wide)
        own_ref[:, a * sep_rows : (a + 1) * sep_rows] = spread
    out_ref[:, :sep_rows] = wide.astype(bf16)
    for a in range(levels - 1):
        columns = pl.ds(sep_rows + a * panel_rows, panel_rows)
        out_ref[:, columns] = jnp.where(wide_level <= a, terms[a + 1], terms[a]).astype(bf16)


def leaf_panel(first_carry_ref, level, panel_rows):
    rows = first_carry_ref.shape[0]
    notes = first_carry_ref[rows - NOTE_ROWS :, :panel_rows].astype(f32)
    return notes[level : level + 1]


def hand_on_kernel(step, sep_rows, own_ref, received_ref, carry_ref):
    lower = ((lax.axis_index("leaf") >> step) & 1) == 0
    following = jnp.where(lower, received_ref[...], own_ref[...])
    skipped = own_ref.shape[1] - carry_ref.shape[1]
    carry_ref[:, :sep_rows] = following[:, :sep_rows]
    if carry_ref.shape[1] > sep_rows:
        carry_ref[:, sep_rows:] = following[:, sep_rows + skipped :]


def keep_kernel(step, own_ref, received_ref, *refs):
    lower = ((lax.axis_index("leaf") >> step) & 1) == 0
    refs[-1][...] = jnp.where(lower, own_ref[...], received_ref[...])


class Factor:
    def __init__(self, own_ref, other_ref, sep_rows, panel_rows):
        self.refs = own_ref, other_ref
        self.sep_rows, self.panel_rows = sep_rows, panel_rows
        self.half = own_ref.shape[0] - NOTE_ROWS

    def columns(self, start, size):
        own, other = (ref[: self.half, start : start + size] for ref in self.refs)
        upper = upper_part() == 1
        return jnp.concatenate([jnp.where(upper, other, own), jnp.where(upper, own, other)], axis=0)

    def inverse(self):
        return self.columns(0, self.sep_rows)

    def updates(self, count):
        return self.columns(self.sep_rows, count * self.panel_rows)

    def panel(self, index):
        start = self.sep_rows + index * self.panel_rows
        notes = self.refs[0][self.half : self.half + NOTE_ROWS, start : start + self.panel_rows]
        return notes.astype(f32)[:1]


def spread_first(message_ref, arrived_ref, wide_level, levels, sep_rows, panel_rows):
    count = sep_rows // panel_rows
    wide = message_ref[:, :sep_rows].astype(f32)
    sums = []
    for level in range(levels):
        value = wide
        panel = leaf_panel(arrived_ref, level, panel_rows)
        for a, here in ((level - 1, wide_level < level), (level, wide_level > level)):
            if 0 <= a < levels - 1:
                columns = pl.ds(sep_rows + a * panel_rows, panel_rows)
                narrow = placed(message_ref[:, columns].astype(f32), panel, count)
                value = jnp.where(here, narrow, value)
        sums.append(value)
    return sums


def solve_up(pending, factor):
    count = factor.sep_rows // factor.panel_rows
    solved = dot_t((-pending[0]).astype(bf16), factor.inverse())
    others = []
    if len(pending) > 1:
        updates = dot(solved.astype(bf16), factor.updates(len(pending) - 1))
        for a, value in enumerate(pending[1:]):
            update = updates[:, a * factor.panel_rows : (a + 1) * factor.panel_rows]
            others.append(value + placed(update, factor.panel(a), count))
    return solved, others


def sums_of(own_ref, received):
    sep_rows = received[0].shape[1]
    return [
        own_ref[:, a * sep_rows : (a + 1) * sep_rows] + value for a, value in enumerate(received)
    ]


def parts_of(ref, sep_rows):
    return [ref[:, low : low + sep_rows].astype(f32) for low in range(0, ref.shape[1], sep_rows)]


def up_kernel(levels, now, panel_rows, own_ref, received_ref, factor_ref, other_ref, *refs):
    solved_ref, sums_ref, out_ref = refs[-3:]
    sep_rows = solved_ref.shape[1]
    if now == 0:
        partner = jnp.minimum(own_level(lax.axis_index("leaf") ^ 1, levels), levels - 1)
        received = spread_first(received_ref, refs[0], partner, levels, sep_rows, panel_rows)
    else:
        received = parts_of(received_ref, sep_rows)
    factor = Factor(factor_ref, other_ref, sep_rows, panel_rows)
    solved, others = solve_up(sums_of(own_ref, received), factor)
    solved_ref[...] = solved
    for a, value in enumerate(others):
        sums_ref[:, a * sep_rows : (a + 1) * sep_rows] = value
        out_ref[:, a * sep_rows : (a + 1) * sep_rows] = value.astype(bf16)


def down_kernel(levels, *refs):
    panel_hbm, own_ref, received_ref, leaf_solved_ref, update_ref, inverse_ref = refs[:6]
    factor_refs = refs[6 : 6 + 2 * levels]
    solved_refs = refs[6 + 2 * levels : 5 + 3 * levels]
    leaf_out_hbm, sep_out_hbm, work_ref, leaf_out_ref, sep_out_ref, panel_ref, sems = refs[
        5 + 3 * levels :
    ]
    copy = pltpu.make_async_copy(panel_hbm, panel_ref, sems.at[0])
    copy.start()
    k = lax.axis_index("leaf")
    rows, sep_rows = own_ref.shape
    panel_rows = update_ref.shape[2]
    count = sep_rows // panel_rows
    level = own_level(k, levels)
    factors = [
        Factor(factor_refs[2 * now], factor_refs[2 * now + 1], sep_rows, panel_rows)
        for now in range(levels)
    ]

    top = levels - 1
    pending = sums_of(own_ref, parts_of(received_ref, sep_rows))
    solved, _ = solve_up(pending, factors[top])
    ancestors = {}
    sep_out = jnp.zeros((rows, sep_rows), f32)
    for now in reversed(range(levels)):
        factor = factors[now]
        residual = solved
        if now < top:
            blocks = [
                picked(ancestors[a], factor.panel(a - now - 1), count).astype(bf16)
                for a in range(now + 1, levels)
            ]
            residual = solved_refs[now][...] - dot_t(
                jnp.concatenate(blocks, axis=1), factor.updates(top - now)
            )
        solution_now = dot(residual.astype(bf16), factor.inverse())
        ancestors[now] = solution_now.astype(bf16).astype(f32)
        sep_out = jnp.where(level == now, solution_now, sep_out)
    sep_out_ref[...] = sep_out
    leaving = [pltpu.make_async_copy(sep_out_ref, sep_out_hbm, sems.at[1])]
    leaving[0].start()

    copy.wait()
    blocks = jnp.concatenate(
        [picked(ancestors[a], panel_ref[0, a], count).astype(bf16) for a in range(levels)], axis=1
    )
    size = inverse_ref.shape[0]
    step = min(256, size)
    for low in range(0, size, step):
        high = low + step
        updates = jnp.concatenate([update_ref[a, low:high, :] for a in range(levels)], axis=1)
        value = leaf_solved_ref[:, low:high] - dot_t(blocks, updates)
        work_ref[:, low:high] = value.astype(bf16)
    for low in range(0, size, step):
        high = low + step
        leaf_out_ref[:, low:high] = dot(work_ref[:, low:], inverse_ref[low:, low:high])
        columns = pl.ds(low, step)
        leaving.append(
            pltpu.make_async_copy(
                leaf_out_ref.at[:, columns],
                leaf_out_hbm.at[:, columns],
                sems.at[len(leaving) + 1],
            )
        )
        leaving[-1].start()
    for copy in leaving:
        copy.wait()


def local(
    leaf_rhs, sep_rhs, leaf_inverse, leaf_update, leaf_panel, sep_inverse, sep_update, sep_panel
):
    levels = lax.axis_size("leaf").bit_length() - 1
    sep_rows = sep_inverse.shape[0]
    scenarios, size = leaf_rhs.shape
    leaf_update, sep_update = leaf_update[0], sep_update[0]
    panel_rows = leaf_update.shape[2]
    panel_smem = pltpu.SMEM(leaf_panel.shape, jnp.int32)
    sems = pltpu.SemaphoreType.DMA((levels + 8 + 3 * (size // min(256, size)),))
    leaf_flops = 2 * scenarios * size * (size + levels * panel_rows)

    def carry_shape(now):
        width = sep_rows + (levels - 1 - now) * panel_rows
        return ((sep_rows // 2 + NOTE_ROWS, width), bf16)

    (carry,) = call(
        partial(pack_kernel, levels),
        [carry_shape(0)],
        (sep_panel, leaf_panel, sep_inverse, sep_update),
        hbm=range(4),
        scratch=[panel_smem, panel_smem, sems],
    )
    arrived = exchange(carry, 1)
    leaf_inverse, leaf_update, leaf_solved, sums, message = call(
        partial(leaf_up_kernel, levels),
        [
            (leaf_inverse.shape, bf16),
            (leaf_update.shape, bf16),
            ((scenarios, size), f32),
            ((scenarios, levels * sep_rows), f32),
            ((scenarios, sep_rows + (levels - 1) * panel_rows), bf16),
        ],
        (carry, leaf_rhs, leaf_inverse, leaf_update, sep_rhs),
        hbm=range(1, 5),
        scratch=[pltpu.VMEM(leaf_rhs.shape, bf16), pltpu.VMEM(sep_rhs.shape, bf16), sems],
        flops=leaf_flops,
    )
    received = exchange(message, 1)
    first = (arrived,)
    factors, solved = [], []
    for now in range(levels):
        pair = (carry, arrived)
        if now + 1 < levels:
            (carry,) = call(
                partial(hand_on_kernel, now, sep_rows), [carry_shape(now + 1)], pair
            )
            arrived = exchange(carry, 2 << now, upward=now + 2 == levels)
            pair += (carry,)
        factors += call(partial(keep_kernel, now), [carry_shape(now)], pair)
        factors.append(exchange(factors[-1], 1, "rhs"))
        if now + 1 == levels:
            break
        extra = (first if now == 0 else ()) + ((arrived,) if now + 2 < levels else ())
        z, sums, message = call(
            partial(up_kernel, levels, now, panel_rows),
            [
                ((scenarios, sep_rows), f32),
                ((scenarios, (levels - 1 - now) * sep_rows), f32),
                ((scenarios, (levels - 1 - now) * sep_rows), bf16),
            ],
            (sums, received, *factors[-2:], *extra),
            flops=2 * scenarios * sep_rows * sep_rows * 2,
        )
        solved.append(z)
        received = exchange(message, 2 << now)
    return call(
        partial(down_kernel, levels),
        [((scenarios, size), f32), ((scenarios, sep_rows), f32)],
        (leaf_panel, sums, received, leaf_solved, leaf_update, leaf_inverse, *factors, *solved),
        hbm=(0,),
        hbm_outs=True,
        scratch=[
            pltpu.VMEM((scenarios, size), bf16),
            pltpu.VMEM((scenarios, size), f32),
            pltpu.VMEM((scenarios, sep_rows), f32),
            panel_smem,
            sems,
        ],
        flops=leaf_flops,
    )


def solution(mesh):
    return jax.shard_map(
        local,
        mesh=mesh,
        in_specs=(
            P("rhs", "leaf"),
            P("rhs", "leaf"),
            P("leaf", None),
            P("leaf", None, None, None),
            P("leaf", None),
            P("leaf", None),
            P("leaf", None, None, None),
            P("leaf", None),
        ),
        out_specs=(P("rhs", "leaf"), P("rhs", "leaf")),
        check_vma=False,
    )
```

```python
from functools import partial

import jax
import jax.numpy as jnp
from jax import lax
from jax.experimental import pallas as pl
from jax.experimental.pallas import tpu as pltpu
from jax.sharding import PartitionSpec as P

NOTE_ROWS = 16
f32, bf16 = jnp.float32, jnp.bfloat16


def dot(a, b):
    return jnp.dot(a, b, preferred_element_type=f32)


def dot_t(a, b):
    return lax.dot_general(a, b, (((1,), (1,)), ((), ())), preferred_element_type=f32)


def own_level(k, levels):
    level = jnp.int32(0)
    for bit in range(levels):
        low = (2 << bit) - 1
        level = jnp.where((k & low) == low, bit + 1, level)
    return level


def placed(block, panel, count):
    return jnp.concatenate(
        [jnp.where(panel == p, block, jnp.zeros_like(block)) for p in range(count)], axis=1
    )


def picked(vectors, panel, count):
    width = vectors.shape[1] // count
    result = vectors[:, :width]
    for p in range(1, count):
        result = jnp.where(panel == p, vectors[:, p * width : (p + 1) * width], result)
    return result


def call(kernel, outs, args, hbm=(), hbm_outs=False, scratch=(), flops=0):
    def bytes_of(arrays):
        return sum(a.size * a.dtype.itemsize for a in arrays)

    outs = [jax.ShapeDtypeStruct(shape, dtype) for shape, dtype in outs]
    args = [
        pltpu.with_memory_space_constraint(arg, pltpu.HBM) if i in hbm else arg
        for i, arg in enumerate(args)
    ]
    return pl.pallas_call(
        kernel,
        out_shape=outs,
        in_specs=[
            pl.BlockSpec(memory_space=pltpu.HBM if i in hbm else pltpu.VMEM)
            for i in range(len(args))
        ],
        out_specs=[pl.BlockSpec(memory_space=pltpu.HBM if hbm_outs else pltpu.VMEM) for _ in outs],
        scratch_shapes=scratch,
        compiler_params=pltpu.CompilerParams(vmem_limit_bytes=40 << 20),
        cost_estimate=pl.CostEstimate(
            flops=flops, bytes_accessed=bytes_of(args) + bytes_of(outs), transcendentals=0
        ),
    )(*args)


def exchange(block, distance, axis="leaf", upward=False):
    route = [(i, i ^ distance) for i in range(lax.axis_size(axis))]
    return lax.ppermute(block, axis, [pair for pair in route if not upward or pair[0] < pair[1]])


def upper_part():
    return lax.axis_index("rhs") & 1


def pack_kernel(
    levels,
    sep_panel_hbm,
    leaf_panel_hbm,
    sep_inverse_hbm,
    sep_update_hbm,
    carry_ref,
    sep_panel_ref,
    leaf_panel_ref,
    sems,
):
    sep_rows, panel_rows = sep_inverse_hbm.shape[1], sep_update_hbm.shape[2]
    half = sep_rows // 2
    copies = []

    def bring(source, target):
        copies.append(pltpu.make_async_copy(source, target, sems.at[len(copies)]))
        copies[-1].start()

    bring(sep_panel_hbm, sep_panel_ref)
    bring(leaf_panel_hbm, leaf_panel_ref)
    rows = pl.ds(pl.multiple_of(upper_part() * half, half), half)
    bring(sep_inverse_hbm.at[rows], carry_ref.at[pl.ds(0, half), pl.ds(0, sep_rows)])
    for a in range(1, levels):
        columns = pl.ds(sep_rows + (a - 1) * panel_rows, panel_rows)
        bring(sep_update_hbm.at[a, rows], carry_ref.at[pl.ds(0, half), columns])

    copies[0].wait()
    copies[1].wait()
    row = lax.broadcasted_iota(jnp.int32, (NOTE_ROWS, sep_rows), 0)
    notes = jnp.zeros((NOTE_ROWS, sep_rows), f32)
    for a in range(levels):
        notes = jnp.where(row == a, leaf_panel_ref[0, a].astype(f32), notes)
    carry_ref[half:, :sep_rows] = notes.astype(bf16)
    for a in range(1, levels):
        columns = pl.ds(sep_rows + (a - 1) * panel_rows, panel_rows)
        carry_ref[half:, columns] = jnp.full(
            (NOTE_ROWS, panel_rows), sep_panel_ref[0, a].astype(f32)
        ).astype(bf16)
    for copy in copies[2:]:
        copy.wait()


def leaf_up_kernel(
    levels,
    carry_ref,
    rhs_hbm,
    inverse_hbm,
    update_hbm,
    sep_rhs_hbm,
    inverse_ref,
    update_ref,
    solved_ref,
    own_ref,
    out_ref,
    rhs_ref,
    sep_rhs_ref,
    sems,
):
    k = lax.axis_index("leaf")
    sep_rows = sep_rhs_ref.shape[1]
    size, panel_rows = inverse_ref.shape[0], update_ref.shape[2]
    count = sep_rows // panel_rows
    step = min(256, size)
    lows = range(0, size, step)
    copies = []

    def bring(source, target):
        copies.append(pltpu.make_async_copy(source, target, sems.at[len(copies)]))
        copies[-1].start()

    bring(rhs_hbm, rhs_ref)
    for low in lows:
        block = (pl.ds(low, step), pl.ds(0, low + step))
        bring(inverse_hbm.at[block], inverse_ref.at[block])
    bring(update_hbm, update_ref)
    bring(sep_rhs_hbm, sep_rhs_ref)

    def solve(low):
        high = low + step
        value = dot_t(rhs_ref[:, :high], inverse_ref[low:high, :high])
        solved_ref[:, low:high] = value
        return value.astype(bf16)

    early = len(copies) - 3
    for copy in copies[:early]:
        copy.wait()
    rounded = [solve(low) for low in lows[:-1]]
    for copy in copies[early:]:
        copy.wait()
    rounded.append(solve(lows[-1]))
    updates = jnp.concatenate([update_ref[a] for a in range(levels)], axis=1)
    together = dot(jnp.concatenate(rounded, axis=1), updates)
    terms = [together[:, a * panel_rows : (a + 1) * panel_rows] for a in range(levels)]
    level = own_level(k, levels)
    wide_level = jnp.minimum(level, levels - 1)
    rhs = jnp.where(level < levels, sep_rhs_ref[...].astype(f32), 0.0)
    wide = jnp.zeros(rhs.shape, f32)
    for a in range(levels):
        spread = placed(terms[a], leaf_panel(carry_ref, a, panel_rows), count)
        spread = jnp.where(wide_level == a, spread - rhs, spread)
        wide = jnp.where(wide_level == a, spread, wide)
        own_ref[:, a * sep_rows : (a + 1) * sep_rows] = spread
    out_ref[:, :sep_rows] = wide.astype(bf16)
    for a in range(levels - 1):
        columns = pl.ds(sep_rows + a * panel_rows, panel_rows)
        out_ref[:, columns] = jnp.where(wide_level <= a, terms[a + 1], terms[a]).astype(bf16)


def leaf_panel(first_carry_ref, level, panel_rows):
    rows = first_carry_ref.shape[0]
    notes = first_carry_ref[rows - NOTE_ROWS :, :panel_rows].astype(f32)
    return notes[level : level + 1]


def hand_on_kernel(step, sep_rows, own_ref, received_ref, carry_ref):
    lower = ((lax.axis_index("leaf") >> step) & 1) == 0
    following = jnp.where(lower, received_ref[...], own_ref[...])
    skipped = own_ref.shape[1] - carry_ref.shape[1]
    carry_ref[:, :sep_rows] = following[:, :sep_rows]
    if carry_ref.shape[1] > sep_rows:
        carry_ref[:, sep_rows:] = following[:, sep_rows + skipped :]


def keep_kernel(step, own_ref, received_ref, *refs):
    lower = ((lax.axis_index("leaf") >> step) & 1) == 0
    refs[-1][...] = jnp.where(lower, own_ref[...], received_ref[...])


class Factor:
    def __init__(self, own_ref, other_ref, sep_rows, panel_rows):
        self.refs = own_ref, other_ref
        self.sep_rows, self.panel_rows = sep_rows, panel_rows
        self.half = own_ref.shape[0] - NOTE_ROWS

    def columns(self, start, size):
        own, other = (ref[: self.half, start : start + size] for ref in self.refs)
        upper = upper_part() == 1
        return jnp.concatenate([jnp.where(upper, other, own), jnp.where(upper, own, other)], axis=0)

    def inverse(self):
        return self.columns(0, self.sep_rows)

    def updates(self, count):
        return self.columns(self.sep_rows, count * self.panel_rows)

    def panel(self, index):
        start = self.sep_rows + index * self.panel_rows
        notes = self.refs[0][self.half : self.half + NOTE_ROWS, start : start + self.panel_rows]
        return notes.astype(f32)[:1]


def spread_first(message_ref, arrived_ref, wide_level, levels, sep_rows, panel_rows):
    count = sep_rows // panel_rows
    wide = message_ref[:, :sep_rows].astype(f32)
    sums = []
    for level in range(levels):
        value = wide
        panel = leaf_panel(arrived_ref, level, panel_rows)
        for a, here in ((level - 1, wide_level < level), (level, wide_level > level)):
            if 0 <= a < levels - 1:
                columns = pl.ds(sep_rows + a * panel_rows, panel_rows)
                narrow = placed(message_ref[:, columns].astype(f32), panel, count)
                value = jnp.where(here, narrow, value)
        sums.append(value)
    return sums


def solve_up(pending, factor):
    count = factor.sep_rows // factor.panel_rows
    solved = dot_t((-pending[0]).astype(bf16), factor.inverse())
    others = []
    if len(pending) > 1:
        updates = dot(solved.astype(bf16), factor.updates(len(pending) - 1))
        for a, value in enumerate(pending[1:]):
            update = updates[:, a * factor.panel_rows : (a + 1) * factor.panel_rows]
            others.append(value + placed(update, factor.panel(a), count))
    return solved, others


def sums_of(own_ref, received):
    sep_rows = received[0].shape[1]
    return [
        own_ref[:, a * sep_rows : (a + 1) * sep_rows] + value for a, value in enumerate(received)
    ]


def parts_of(ref, sep_rows):
    return [ref[:, low : low + sep_rows].astype(f32) for low in range(0, ref.shape[1], sep_rows)]


def up_kernel(levels, now, panel_rows, own_ref, received_ref, factor_ref, other_ref, *refs):
    solved_ref, sums_ref, out_ref = refs[-3:]
    sep_rows = solved_ref.shape[1]
    if now == 0:
        partner = jnp.minimum(own_level(lax.axis_index("leaf") ^ 1, levels), levels - 1)
        received = spread_first(received_ref, refs[0], partner, levels, sep_rows, panel_rows)
    else:
        received = parts_of(received_ref, sep_rows)
    factor = Factor(factor_ref, other_ref, sep_rows, panel_rows)
    solved, others = solve_up(sums_of(own_ref, received), factor)
    solved_ref[...] = solved
    for a, value in enumerate(others):
        sums_ref[:, a * sep_rows : (a + 1) * sep_rows] = value
        out_ref[:, a * sep_rows : (a + 1) * sep_rows] = value.astype(bf16)


def prepare_kernel(levels, solved_ref, update_ref, inverse_ref, base_ref, folded_ref):
    size, panel_rows = inverse_ref.shape[0], update_ref.shape[2]
    step = min(256, size)
    for low in range(0, size, step):
        high = low + step
        solved = solved_ref[:, low:]
        coarse = solved.astype(bf16)
        fine = (solved - coarse.astype(f32)).astype(bf16)
        block = inverse_ref[low:, low:high]
        base_ref[:, low:high] = dot(coarse, block) + dot(fine, block)
        for a in range(levels):
            folded_ref[a * panel_rows : (a + 1) * panel_rows, low:high] = lax.dot_general(
                update_ref[a, low:, :],
                block,
                (((0,), (0,)), ((), ())),
                preferred_element_type=f32,
            ).astype(bf16)


def down_kernel(levels, *refs):
    panel_hbm, own_ref, received_ref, base_ref, folded_ref = refs[:5]
    factor_refs = refs[5 : 5 + 2 * levels]
    solved_refs = refs[5 + 2 * levels : 4 + 3 * levels]
    leaf_out_hbm, sep_out_hbm, leaf_out_ref, sep_out_ref, panel_ref, sems = refs[4 + 3 * levels :]
    copy = pltpu.make_async_copy(panel_hbm, panel_ref, sems.at[0])
    copy.start()
    k = lax.axis_index("leaf")
    rows, sep_rows = own_ref.shape
    panel_rows = folded_ref.shape[0] // levels
    count = sep_rows // panel_rows
    level = own_level(k, levels)
    factors = [
        Factor(factor_refs[2 * now], factor_refs[2 * now + 1], sep_rows, panel_rows)
        for now in range(levels)
    ]

    top = levels - 1
    pending = sums_of(own_ref, parts_of(received_ref, sep_rows))
    solved, _ = solve_up(pending, factors[top])
    ancestors = {}
    sep_out = jnp.zeros((rows, sep_rows), f32)
    for now in reversed(range(levels)):
        factor = factors[now]
        residual = solved
        if now < top:
            blocks = [
                picked(ancestors[a], factor.panel(a - now - 1), count).astype(bf16)
                for a in range(now + 1, levels)
            ]
            residual = solved_refs[now][...] - dot_t(
                jnp.concatenate(blocks, axis=1), factor.updates(top - now)
            )
        solution_now = dot(residual.astype(bf16), factor.inverse())
        ancestors[now] = solution_now.astype(bf16).astype(f32)
        sep_out = jnp.where(level == now, solution_now, sep_out)
    sep_out_ref[...] = sep_out
    leaving = [pltpu.make_async_copy(sep_out_ref, sep_out_hbm, sems.at[1])]
    leaving[0].start()

    copy.wait()
    blocks = jnp.concatenate(
        [picked(ancestors[a], panel_ref[0, a], count).astype(bf16) for a in range(levels)], axis=1
    )
    size = folded_ref.shape[1]
    step = min(256, size)
    for low in range(0, size, step):
        high = low + step
        leaf_out_ref[:, low:high] = base_ref[:, low:high] - dot(blocks, folded_ref[:, low:high])
        columns = pl.ds(low, step)
        leaving.append(
            pltpu.make_async_copy(
                leaf_out_ref.at[:, columns],
                leaf_out_hbm.at[:, columns],
                sems.at[len(leaving) + 1],
            )
        )
        leaving[-1].start()
    for copy in leaving:
        copy.wait()


def local(
    leaf_rhs, sep_rhs, leaf_inverse, leaf_update, leaf_panel, sep_inverse, sep_update, sep_panel
):
    levels = lax.axis_size("leaf").bit_length() - 1
    sep_rows = sep_inverse.shape[0]
    scenarios, size = leaf_rhs.shape
    leaf_update, sep_update = leaf_update[0], sep_update[0]
    panel_rows = leaf_update.shape[2]
    panel_smem = pltpu.SMEM(leaf_panel.shape, jnp.int32)
    sems = pltpu.SemaphoreType.DMA((levels + 8 + 3 * (size // min(256, size)),))
    leaf_flops = 2 * scenarios * size * (size + levels * panel_rows)

    def carry_shape(now):
        width = sep_rows + (levels - 1 - now) * panel_rows
        return ((sep_rows // 2 + NOTE_ROWS, width), bf16)

    (carry,) = call(
        partial(pack_kernel, levels),
        [carry_shape(0)],
        (sep_panel, leaf_panel, sep_inverse, sep_update),
        hbm=range(4),
        scratch=[panel_smem, panel_smem, sems],
    )
    arrived = exchange(carry, 1)
    leaf_inverse, leaf_update, leaf_solved, sums, message = call(
        partial(leaf_up_kernel, levels),
        [
            (leaf_inverse.shape, bf16),
            (leaf_update.shape, bf16),
            ((scenarios, size), f32),
            ((scenarios, levels * sep_rows), f32),
            ((scenarios, sep_rows + (levels - 1) * panel_rows), bf16),
        ],
        (carry, leaf_rhs, leaf_inverse, leaf_update, sep_rhs),
        hbm=range(1, 5),
        scratch=[pltpu.VMEM(leaf_rhs.shape, bf16), pltpu.VMEM(sep_rhs.shape, bf16), sems],
        flops=leaf_flops,
    )
    received = exchange(message, 1)
    base, folded = call(
        partial(prepare_kernel, levels),
        [((scenarios, size), f32), ((levels * panel_rows, size), bf16)],
        (leaf_solved, leaf_update, leaf_inverse),
        flops=2 * leaf_flops,
    )
    first = (arrived,)
    factors, solved = [], []
    for now in range(levels):
        pair = (carry, arrived)
        if now + 1 < levels:
            (carry,) = call(
                partial(hand_on_kernel, now, sep_rows), [carry_shape(now + 1)], pair
            )
            arrived = exchange(carry, 2 << now, upward=now + 2 == levels)
            pair += (carry,)
        factors += call(partial(keep_kernel, now), [carry_shape(now)], pair)
        factors.append(exchange(factors[-1], 1, "rhs"))
        if now + 1 == levels:
            break
        extra = (*first, folded) if now == 0 else ()
        extra += (arrived,) if now + 2 < levels else ()
        z, sums, message = call(
            partial(up_kernel, levels, now, panel_rows),
            [
                ((scenarios, sep_rows), f32),
                ((scenarios, (levels - 1 - now) * sep_rows), f32),
                ((scenarios, (levels - 1 - now) * sep_rows), bf16),
            ],
            (sums, received, *factors[-2:], *extra),
            flops=2 * scenarios * sep_rows * sep_rows * 2,
        )
        solved.append(z)
        received = exchange(message, 2 << now)
    return call(
        partial(down_kernel, levels),
        [((scenarios, size), f32), ((scenarios, sep_rows), f32)],
        (leaf_panel, sums, received, base, folded, *factors, *solved),
        hbm=(0,),
        hbm_outs=True,
        scratch=[
            pltpu.VMEM((scenarios, size), f32),
            pltpu.VMEM((scenarios, sep_rows), f32),
            panel_smem,
            sems,
        ],
        flops=leaf_flops,
    )


def solution(mesh):
    return jax.shard_map(
        local,
        mesh=mesh,
        in_specs=(
            P("rhs", "leaf"),
            P("rhs", "leaf"),
            P("leaf", None),
            P("leaf", None, None, None),
            P("leaf", None),
            P("leaf", None),
            P("leaf", None, None, None),
            P("leaf", None),
        ),
        out_specs=(P("rhs", "leaf"), P("rhs", "leaf")),
        check_vma=False,
    )
```

```python
from functools import partial

import jax
import jax.numpy as jnp
from jax import lax
from jax.experimental import pallas as pl
from jax.experimental.pallas import tpu as pltpu
from jax.sharding import PartitionSpec as P

NOTE_ROWS = 16
f32, bf16 = jnp.float32, jnp.bfloat16


def dot(a, b):
    return jnp.dot(a, b, preferred_element_type=f32)


def dot_t(a, b):
    return lax.dot_general(a, b, (((1,), (1,)), ((), ())), preferred_element_type=f32)


def own_level(k, levels):
    level = jnp.int32(0)
    for bit in range(levels):
        low = (2 << bit) - 1
        level = jnp.where((k & low) == low, bit + 1, level)
    return level


def placed(block, panel, count):
    return jnp.concatenate(
        [jnp.where(panel == p, block, jnp.zeros_like(block)) for p in range(count)], axis=1
    )


def picked(vectors, panel, count):
    width = vectors.shape[1] // count
    result = vectors[:, :width]
    for p in range(1, count):
        result = jnp.where(panel == p, vectors[:, p * width : (p + 1) * width], result)
    return result


def call(kernel, outs, args, hbm=(), hbm_outs=False, scratch=(), flops=0):
    def bytes_of(arrays):
        return sum(a.size * a.dtype.itemsize for a in arrays)

    outs = [jax.ShapeDtypeStruct(shape, dtype) for shape, dtype in outs]
    args = [
        pltpu.with_memory_space_constraint(arg, pltpu.HBM) if i in hbm else arg
        for i, arg in enumerate(args)
    ]
    return pl.pallas_call(
        kernel,
        out_shape=outs,
        in_specs=[
            pl.BlockSpec(memory_space=pltpu.HBM if i in hbm else pltpu.VMEM)
            for i in range(len(args))
        ],
        out_specs=[pl.BlockSpec(memory_space=pltpu.HBM if hbm_outs else pltpu.VMEM) for _ in outs],
        scratch_shapes=scratch,
        compiler_params=pltpu.CompilerParams(vmem_limit_bytes=40 << 20),
        cost_estimate=pl.CostEstimate(
            flops=flops, bytes_accessed=bytes_of(args) + bytes_of(outs), transcendentals=0
        ),
    )(*args)


def exchange(block, distance, axis="leaf", upward=False):
    route = [(i, i ^ distance) for i in range(lax.axis_size(axis))]
    return lax.ppermute(block, axis, [pair for pair in route if not upward or pair[0] < pair[1]])


def upper_part():
    return lax.axis_index("rhs") & 1


def pack_kernel(
    levels,
    sep_panel_hbm,
    leaf_panel_hbm,
    sep_inverse_hbm,
    sep_update_hbm,
    carry_ref,
    sep_panel_ref,
    leaf_panel_ref,
    sems,
):
    sep_rows, panel_rows = sep_inverse_hbm.shape[1], sep_update_hbm.shape[2]
    half = sep_rows // 2
    copies = []

    def bring(source, target):
        copies.append(pltpu.make_async_copy(source, target, sems.at[len(copies)]))
        copies[-1].start()

    bring(sep_panel_hbm, sep_panel_ref)
    bring(leaf_panel_hbm, leaf_panel_ref)
    rows = pl.ds(pl.multiple_of(upper_part() * half, half), half)
    bring(sep_inverse_hbm.at[rows], carry_ref.at[pl.ds(0, half), pl.ds(0, sep_rows)])
    for a in range(1, levels):
        columns = pl.ds(sep_rows + (a - 1) * panel_rows, panel_rows)
        bring(sep_update_hbm.at[a, rows], carry_ref.at[pl.ds(0, half), columns])

    copies[0].wait()
    copies[1].wait()
    row = lax.broadcasted_iota(jnp.int32, (NOTE_ROWS, sep_rows), 0)
    notes = jnp.zeros((NOTE_ROWS, sep_rows), f32)
    for a in range(levels):
        notes = jnp.where(row == a, leaf_panel_ref[0, a].astype(f32), notes)
    carry_ref[half:, :sep_rows] = notes.astype(bf16)
    for a in range(1, levels):
        columns = pl.ds(sep_rows + (a - 1) * panel_rows, panel_rows)
        carry_ref[half:, columns] = jnp.full(
            (NOTE_ROWS, panel_rows), sep_panel_ref[0, a].astype(f32)
        ).astype(bf16)
    for copy in copies[2:]:
        copy.wait()


def leaf_up_kernel(
    levels,
    carry_ref,
    rhs_hbm,
    inverse_hbm,
    update_hbm,
    sep_rhs_hbm,
    inverse_ref,
    update_ref,
    solved_ref,
    own_ref,
    out_ref,
    rhs_ref,
    sep_rhs_ref,
    sems,
):
    k = lax.axis_index("leaf")
    sep_rows = sep_rhs_ref.shape[1]
    size, panel_rows = inverse_ref.shape[0], update_ref.shape[2]
    count = sep_rows // panel_rows
    step = min(256, size)
    lows = range(0, size, step)
    copies = []

    def bring(source, target):
        copies.append(pltpu.make_async_copy(source, target, sems.at[len(copies)]))
        copies[-1].start()

    bring(rhs_hbm, rhs_ref)
    for low in lows:
        block = (pl.ds(low, step), pl.ds(0, low + step))
        bring(inverse_hbm.at[block], inverse_ref.at[block])
    bring(update_hbm, update_ref)
    bring(sep_rhs_hbm, sep_rhs_ref)

    def solve(low):
        high = low + step
        value = dot_t(rhs_ref[:, :high], inverse_ref[low:high, :high])
        solved_ref[:, low:high] = value
        return value.astype(bf16)

    early = len(copies) - 3
    for copy in copies[:early]:
        copy.wait()
    rounded = [solve(low) for low in lows[:-1]]
    for copy in copies[early:]:
        copy.wait()
    rounded.append(solve(lows[-1]))
    updates = jnp.concatenate([update_ref[a] for a in range(levels)], axis=1)
    together = dot(jnp.concatenate(rounded, axis=1), updates)
    terms = [together[:, a * panel_rows : (a + 1) * panel_rows] for a in range(levels)]
    level = own_level(k, levels)
    wide_level = jnp.minimum(level, levels - 1)
    rhs = jnp.where(level < levels, sep_rhs_ref[...].astype(f32), 0.0)
    wide = jnp.zeros(rhs.shape, f32)
    for a in range(levels):
        spread = placed(terms[a], leaf_panel(carry_ref, a, panel_rows), count)
        spread = jnp.where(wide_level == a, spread - rhs, spread)
        wide = jnp.where(wide_level == a, spread, wide)
        own_ref[:, a * sep_rows : (a + 1) * sep_rows] = spread
    out_ref[:, :sep_rows] = wide.astype(bf16)
    for a in range(levels - 1):
        columns = pl.ds(sep_rows + a * panel_rows, panel_rows)
        out_ref[:, columns] = jnp.where(wide_level <= a, terms[a + 1], terms[a]).astype(bf16)


def leaf_panel(first_carry_ref, level, panel_rows):
    rows = first_carry_ref.shape[0]
    notes = first_carry_ref[rows - NOTE_ROWS :, :panel_rows].astype(f32)
    return notes[level : level + 1]


def hand_on_kernel(step, sep_rows, own_ref, received_ref, carry_ref):
    lower = ((lax.axis_index("leaf") >> step) & 1) == 0
    following = jnp.where(lower, received_ref[...], own_ref[...])
    skipped = own_ref.shape[1] - carry_ref.shape[1]
    carry_ref[:, :sep_rows] = following[:, :sep_rows]
    if carry_ref.shape[1] > sep_rows:
        carry_ref[:, sep_rows:] = following[:, sep_rows + skipped :]


def keep_kernel(step, own_ref, received_ref, *refs):
    lower = ((lax.axis_index("leaf") >> step) & 1) == 0
    refs[-1][...] = jnp.where(lower, own_ref[...], received_ref[...])


class Factor:
    def __init__(self, own_ref, other_ref, sep_rows, panel_rows):
        self.refs = own_ref, other_ref
        self.sep_rows, self.panel_rows = sep_rows, panel_rows
        self.half = own_ref.shape[0] - NOTE_ROWS

    def columns(self, start, size):
        own, other = (ref[: self.half, start : start + size] for ref in self.refs)
        upper = upper_part() == 1
        return jnp.concatenate([jnp.where(upper, other, own), jnp.where(upper, own, other)], axis=0)

    def inverse(self):
        return self.columns(0, self.sep_rows)

    def updates(self, count):
        return self.columns(self.sep_rows, count * self.panel_rows)

    def panel(self, index):
        start = self.sep_rows + index * self.panel_rows
        notes = self.refs[0][self.half : self.half + NOTE_ROWS, start : start + self.panel_rows]
        return notes.astype(f32)[:1]


def spread_first(message_ref, arrived_ref, wide_level, levels, sep_rows, panel_rows):
    count = sep_rows // panel_rows
    wide = message_ref[:, :sep_rows].astype(f32)
    sums = []
    for level in range(levels):
        value = wide
        panel = leaf_panel(arrived_ref, level, panel_rows)
        for a, here in ((level - 1, wide_level < level), (level, wide_level > level)):
            if 0 <= a < levels - 1:
                columns = pl.ds(sep_rows + a * panel_rows, panel_rows)
                narrow = placed(message_ref[:, columns].astype(f32), panel, count)
                value = jnp.where(here, narrow, value)
        sums.append(value)
    return sums


def solve_up(pending, factor):
    count = factor.sep_rows // factor.panel_rows
    solved = dot_t((-pending[0]).astype(bf16), factor.inverse())
    others = []
    if len(pending) > 1:
        updates = dot(solved.astype(bf16), factor.updates(len(pending) - 1))
        for a, value in enumerate(pending[1:]):
            update = updates[:, a * factor.panel_rows : (a + 1) * factor.panel_rows]
            others.append(value + placed(update, factor.panel(a), count))
    return solved, others


def sums_of(own_ref, received):
    sep_rows = received[0].shape[1]
    return [
        own_ref[:, a * sep_rows : (a + 1) * sep_rows] + value for a, value in enumerate(received)
    ]


def parts_of(ref, sep_rows):
    return [ref[:, low : low + sep_rows].astype(f32) for low in range(0, ref.shape[1], sep_rows)]


def up_kernel(levels, now, panel_rows, own_ref, received_ref, factor_ref, other_ref, *refs):
    solved_ref, sums_ref, out_ref = refs[-3:]
    sep_rows = solved_ref.shape[1]
    if now == 0:
        partner = jnp.minimum(own_level(lax.axis_index("leaf") ^ 1, levels), levels - 1)
        received = spread_first(received_ref, refs[0], partner, levels, sep_rows, panel_rows)
    else:
        received = parts_of(received_ref, sep_rows)
    factor = Factor(factor_ref, other_ref, sep_rows, panel_rows)
    solved, others = solve_up(sums_of(own_ref, received), factor)
    solved_ref[...] = solved
    for a, value in enumerate(others):
        sums_ref[:, a * sep_rows : (a + 1) * sep_rows] = value
        out_ref[:, a * sep_rows : (a + 1) * sep_rows] = value.astype(bf16)


def prepare_kernel(levels, solved_ref, update_ref, inverse_ref, base_ref, folded_ref):
    size, panel_rows = inverse_ref.shape[0], update_ref.shape[2]
    step = min(256, size)
    for low in range(0, size, step):
        high = low + step
        coarse, fine = two_parts(solved_ref[:, low:])
        block = inverse_ref[low:, low:high]
        base_ref[:, low:high] = dot(coarse, block) + dot(fine, block)
        for a in range(levels):
            folded_ref[a * panel_rows : (a + 1) * panel_rows, low:high] = contract_rows(
                update_ref[a, low:, :], block
            ).astype(bf16)


def two_parts(value):
    coarse = value.astype(bf16)
    return coarse, (value - coarse.astype(f32)).astype(bf16)


def contract_rows(a, b):
    return lax.dot_general(a, b, (((0,), (0,)), ((), ())), preferred_element_type=f32)


def fold_kernel(levels, panel_rows, *refs):
    below = levels - 1
    for now in range(below):
        own_ref, other_ref, solved_ref = refs[3 * now : 3 * now + 3]
        base_ref, folded_ref = refs[3 * below + 2 * now : 3 * below + 2 * now + 2]
        factor = Factor(own_ref, other_ref, base_ref.shape[1], panel_rows)
        inverse = factor.inverse()
        coarse, fine = two_parts(solved_ref[...])
        base_ref[...] = dot(coarse, inverse) + dot(fine, inverse)
        folded_ref[...] = contract_rows(factor.updates(below - now), inverse).astype(bf16)


def square_kernel(panel_rows, own_ref, other_ref, coarse_ref, fine_ref):
    inverse = Factor(own_ref, other_ref, coarse_ref.shape[1], panel_rows).inverse()
    coarse_ref[...], fine_ref[...] = two_parts(contract_rows(inverse, inverse))


def down_kernel(levels, *refs):
    carry_ref, own_ref, received_ref, base_ref, folded_ref, coarse_ref, fine_ref = refs[:7]
    below = levels - 1
    factor_refs = refs[7 : 7 + below]
    folds = refs[7 + below : 7 + 3 * below]
    leaf_out_hbm, sep_out_hbm, leaf_out_ref, sep_out_ref, sems = refs[7 + 3 * below :]
    level = own_level(lax.axis_index("leaf"), levels)
    sep_rows = own_ref.shape[1]
    panel_rows = folded_ref.shape[0] // levels
    count = sep_rows // panel_rows

    residual = (-(own_ref[...] + received_ref[...].astype(f32))).astype(bf16)
    solution_now = dot(residual, coarse_ref[...]) + dot(residual, fine_ref[...])
    ancestors = {below: solution_now.astype(bf16).astype(f32)}
    sep_out = jnp.where(level == below, solution_now, 0.0)
    for now in reversed(range(below)):
        factor = Factor(factor_refs[now], None, sep_rows, panel_rows)
        blocks = [
            picked(ancestors[a], factor.panel(a - now - 1), count).astype(bf16)
            for a in range(now + 1, levels)
        ]
        solution_now = folds[2 * now][...] - dot(
            jnp.concatenate(blocks, axis=1), folds[2 * now + 1][...]
        )
        ancestors[now] = solution_now.astype(bf16).astype(f32)
        sep_out = jnp.where(level == now, solution_now, sep_out)
    sep_out_ref[...] = sep_out
    leaving = [pltpu.make_async_copy(sep_out_ref, sep_out_hbm, sems.at[0])]
    leaving[0].start()

    blocks = [
        picked(ancestors[a], leaf_panel(carry_ref, a, panel_rows), count).astype(bf16)
        for a in range(levels)
    ]
    blocks = jnp.concatenate(blocks, axis=1)
    size = folded_ref.shape[1]
    step = min(256, size)
    for low in range(0, size, step):
        high = low + step
        leaf_out_ref[:, low:high] = base_ref[:, low:high] - dot(blocks, folded_ref[:, low:high])
        columns = pl.ds(low, step)
        leaving.append(
            pltpu.make_async_copy(
                leaf_out_ref.at[:, columns],
                leaf_out_hbm.at[:, columns],
                sems.at[len(leaving)],
            )
        )
        leaving[-1].start()
    for copy in leaving:
        copy.wait()


def local(
    leaf_rhs, sep_rhs, leaf_inverse, leaf_update, leaf_panel, sep_inverse, sep_update, sep_panel
):
    levels = lax.axis_size("leaf").bit_length() - 1
    sep_rows = sep_inverse.shape[0]
    scenarios, size = leaf_rhs.shape
    leaf_update, sep_update = leaf_update[0], sep_update[0]
    panel_rows = leaf_update.shape[2]
    panel_smem = pltpu.SMEM(leaf_panel.shape, jnp.int32)
    sems = pltpu.SemaphoreType.DMA((levels + 8 + 3 * (size // min(256, size)),))
    leaf_flops = 2 * scenarios * size * (size + levels * panel_rows)

    def carry_shape(now):
        width = sep_rows + (levels - 1 - now) * panel_rows
        return ((sep_rows // 2 + NOTE_ROWS, width), bf16)

    (carry,) = call(
        partial(pack_kernel, levels),
        [carry_shape(0)],
        (sep_panel, leaf_panel, sep_inverse, sep_update),
        hbm=range(4),
        scratch=[panel_smem, panel_smem, sems],
    )
    first_carry, arrived = carry, exchange(carry, 1)
    leaf_inverse, leaf_update, leaf_solved, sums, message = call(
        partial(leaf_up_kernel, levels),
        [
            (leaf_inverse.shape, bf16),
            (leaf_update.shape, bf16),
            ((scenarios, size), f32),
            ((scenarios, levels * sep_rows), f32),
            ((scenarios, sep_rows + (levels - 1) * panel_rows), bf16),
        ],
        (carry, leaf_rhs, leaf_inverse, leaf_update, sep_rhs),
        hbm=range(1, 5),
        scratch=[pltpu.VMEM(leaf_rhs.shape, bf16), pltpu.VMEM(sep_rhs.shape, bf16), sems],
        flops=leaf_flops,
    )
    received = exchange(message, 1)
    base, folded = call(
        partial(prepare_kernel, levels),
        [((scenarios, size), f32), ((levels * panel_rows, size), bf16)],
        (leaf_solved, leaf_update, leaf_inverse),
        flops=2 * leaf_flops,
    )
    first = (arrived,)
    factors, solved = [], []
    for now in range(levels):
        pair = (carry, arrived)
        if now + 1 < levels:
            (carry,) = call(
                partial(hand_on_kernel, now, sep_rows), [carry_shape(now + 1)], pair
            )
            arrived = exchange(carry, 2 << now, upward=now + 2 == levels)
            pair += (carry,)
        elif levels > 1:
            pair += (message,)
        factors += call(partial(keep_kernel, now), [carry_shape(now)], pair)
        factors.append(exchange(factors[-1], 1, "rhs"))
        if now + 1 == levels:
            break
        extra = (*first, folded) if now == 0 else ()
        extra += (arrived,) if now + 2 < levels else ()
        z, sums, message = call(
            partial(up_kernel, levels, now, panel_rows),
            [
                ((scenarios, sep_rows), f32),
                ((scenarios, (levels - 1 - now) * sep_rows), f32),
                ((scenarios, (levels - 1 - now) * sep_rows), bf16),
            ],
            (sums, received, *factors[-2:], *extra),
            flops=2 * scenarios * sep_rows * sep_rows * 2,
        )
        solved.append(z)
        received = exchange(message, 2 << now)
    below = levels - 1
    triples, shapes = (), []
    for now in range(below):
        triples += (factors[2 * now], factors[2 * now + 1], solved[now])
        shapes += [((scenarios, sep_rows), f32), (((below - now) * panel_rows, sep_rows), bf16)]
    folds = call(
        partial(fold_kernel, levels, panel_rows),
        shapes,
        triples,
        flops=6 * below * scenarios * sep_rows * sep_rows,
    )
    square = call(
        partial(square_kernel, panel_rows),
        [((sep_rows, sep_rows), bf16)] * 2,
        (factors[-2], factors[-1]),
        flops=2 * sep_rows**3,
    )
    return call(
        partial(down_kernel, levels),
        [((scenarios, size), f32), ((scenarios, sep_rows), f32)],
        (first_carry, sums, received, base, folded, *square, *factors[: 2 * below : 2], *folds),
        hbm_outs=True,
        scratch=[
            pltpu.VMEM((scenarios, size), f32),
            pltpu.VMEM((scenarios, sep_rows), f32),
            sems,
        ],
        flops=leaf_flops,
    )


def solution(mesh):
    return jax.shard_map(
        local,
        mesh=mesh,
        in_specs=(
            P("rhs", "leaf"),
            P("rhs", "leaf"),
            P("leaf", None),
            P("leaf", None, None, None),
            P("leaf", None),
            P("leaf", None),
            P("leaf", None, None, None),
            P("leaf", None),
        ),
        out_specs=(P("rhs", "leaf"), P("rhs", "leaf")),
        check_vma=False,
    )
```

```python
from functools import partial

import jax
import jax.numpy as jnp
from jax import lax
from jax.experimental import pallas as pl
from jax.experimental.pallas import tpu as pltpu
from jax.sharding import PartitionSpec as P

NOTE_ROWS = 16
f32, bf16 = jnp.float32, jnp.bfloat16


def dot(a, b):
    return jnp.dot(a, b, preferred_element_type=f32)


def dot_t(a, b):
    return lax.dot_general(a, b, (((1,), (1,)), ((), ())), preferred_element_type=f32)


def own_level(k, levels):
    level = jnp.int32(0)
    for bit in range(levels):
        low = (2 << bit) - 1
        level = jnp.where((k & low) == low, bit + 1, level)
    return level


def placed(block, panel, count):
    return jnp.concatenate(
        [jnp.where(panel == p, block, jnp.zeros_like(block)) for p in range(count)], axis=1
    )


def picked(vectors, panel, count):
    width = vectors.shape[1] // count
    result = vectors[:, :width]
    for p in range(1, count):
        result = jnp.where(panel == p, vectors[:, p * width : (p + 1) * width], result)
    return result


def call(kernel, outs, args, hbm=(), hbm_outs=False, scratch=(), flops=0):
    def bytes_of(arrays):
        return sum(a.size * a.dtype.itemsize for a in arrays)

    outs = [jax.ShapeDtypeStruct(shape, dtype) for shape, dtype in outs]
    args = [
        pltpu.with_memory_space_constraint(arg, pltpu.HBM) if i in hbm else arg
        for i, arg in enumerate(args)
    ]
    return pl.pallas_call(
        kernel,
        out_shape=outs,
        in_specs=[
            pl.BlockSpec(memory_space=pltpu.HBM if i in hbm else pltpu.VMEM)
            for i in range(len(args))
        ],
        out_specs=[pl.BlockSpec(memory_space=pltpu.HBM if hbm_outs else pltpu.VMEM) for _ in outs],
        scratch_shapes=scratch,
        compiler_params=pltpu.CompilerParams(vmem_limit_bytes=40 << 20),
        cost_estimate=pl.CostEstimate(
            flops=flops, bytes_accessed=bytes_of(args) + bytes_of(outs), transcendentals=0
        ),
    )(*args)


def exchange(block, distance, axis="leaf"):
    return lax.ppermute(block, axis, [(i, i ^ distance) for i in range(lax.axis_size(axis))])


def exchange_among(block, distance, members):
    leaves, parts = lax.axis_size("leaf"), lax.axis_size("rhs")
    route = []
    for leaf in range(leaves):
        for part in range(parts):
            target = (leaf ^ distance, part) if leaf in members else (leaf, part ^ 1)
            route.append((leaf * parts + part, target[0] * parts + target[1]))
    return lax.ppermute(block, ("leaf", "rhs"), route)


def upper_part():
    return lax.axis_index("rhs") & 1


def pack_kernel(
    levels,
    sep_panel_hbm,
    leaf_panel_hbm,
    sep_inverse_hbm,
    sep_update_hbm,
    carry_ref,
    sep_panel_ref,
    leaf_panel_ref,
    sems,
):
    sep_rows, panel_rows = sep_inverse_hbm.shape[1], sep_update_hbm.shape[2]
    half = sep_rows // 2
    copies = []

    def bring(source, target):
        copies.append(pltpu.make_async_copy(source, target, sems.at[len(copies)]))
        copies[-1].start()

    bring(sep_panel_hbm, sep_panel_ref)
    bring(leaf_panel_hbm, leaf_panel_ref)
    rows = pl.ds(pl.multiple_of(upper_part() * half, half), half)
    bring(sep_inverse_hbm.at[rows], carry_ref.at[pl.ds(0, half), pl.ds(0, sep_rows)])
    for a in range(1, levels):
        columns = pl.ds(sep_rows + (a - 1) * panel_rows, panel_rows)
        bring(sep_update_hbm.at[a, rows], carry_ref.at[pl.ds(0, half), columns])

    copies[0].wait()
    copies[1].wait()
    row = lax.broadcasted_iota(jnp.int32, (NOTE_ROWS, sep_rows), 0)
    notes = jnp.zeros((NOTE_ROWS, sep_rows), f32)
    for a in range(levels):
        notes = jnp.where(row == a, leaf_panel_ref[0, a].astype(f32), notes)
    carry_ref[half:, :sep_rows] = notes.astype(bf16)
    for a in range(1, levels):
        columns = pl.ds(sep_rows + (a - 1) * panel_rows, panel_rows)
        carry_ref[half:, columns] = jnp.full(
            (NOTE_ROWS, panel_rows), sep_panel_ref[0, a].astype(f32)
        ).astype(bf16)
    for copy in copies[2:]:
        copy.wait()


def leaf_up_kernel(
    levels,
    carry_ref,
    rhs_hbm,
    inverse_hbm,
    update_hbm,
    sep_rhs_hbm,
    inverse_ref,
    update_ref,
    solved_ref,
    own_ref,
    out_ref,
    rhs_ref,
    sep_rhs_ref,
    sems,
):
    k = lax.axis_index("leaf")
    sep_rows = sep_rhs_ref.shape[1]
    size, panel_rows = inverse_ref.shape[0], update_ref.shape[2]
    count = sep_rows // panel_rows
    step = min(256, size)
    lows = range(0, size, step)
    copies = []

    def bring(source, target):
        copies.append(pltpu.make_async_copy(source, target, sems.at[len(copies)]))
        copies[-1].start()

    bring(rhs_hbm, rhs_ref)
    for low in lows:
        block = (pl.ds(low, step), pl.ds(0, low + step))
        bring(inverse_hbm.at[block], inverse_ref.at[block])
    bring(update_hbm, update_ref)
    bring(sep_rhs_hbm, sep_rhs_ref)

    def solve(low):
        high = low + step
        value = dot_t(rhs_ref[:, :high], inverse_ref[low:high, :high])
        solved_ref[:, low:high] = value
        return value.astype(bf16)

    early = len(copies) - 3
    for copy in copies[:early]:
        copy.wait()
    rounded = [solve(low) for low in lows[:-1]]
    for copy in copies[early:]:
        copy.wait()
    rounded.append(solve(lows[-1]))
    updates = jnp.concatenate([update_ref[a] for a in range(levels)], axis=1)
    together = dot(jnp.concatenate(rounded, axis=1), updates)
    terms = [together[:, a * panel_rows : (a + 1) * panel_rows] for a in range(levels)]
    level = own_level(k, levels)
    wide_level = jnp.minimum(level, levels - 1)
    rhs = jnp.where(level < levels, sep_rhs_ref[...].astype(f32), 0.0)
    wide = jnp.zeros(rhs.shape, f32)
    for a in range(levels):
        spread = placed(terms[a], leaf_panel(carry_ref, a, panel_rows), count)
        spread = jnp.where(wide_level == a, spread - rhs, spread)
        wide = jnp.where(wide_level == a, spread, wide)
        own_ref[:, a * sep_rows : (a + 1) * sep_rows] = spread
    out_ref[:, :sep_rows] = wide.astype(bf16)
    for a in range(levels - 1):
        columns = pl.ds(sep_rows + a * panel_rows, panel_rows)
        out_ref[:, columns] = jnp.where(wide_level <= a, terms[a + 1], terms[a]).astype(bf16)


def leaf_panel(first_carry_ref, level, panel_rows):
    rows = first_carry_ref.shape[0]
    notes = first_carry_ref[rows - NOTE_ROWS :, :panel_rows].astype(f32)
    return notes[level : level + 1]


def hand_on_kernel(step, sep_rows, own_ref, received_ref, carry_ref):
    lower = ((lax.axis_index("leaf") >> step) & 1) == 0
    following = jnp.where(lower, received_ref[...], own_ref[...])
    skipped = own_ref.shape[1] - carry_ref.shape[1]
    carry_ref[:, :sep_rows] = following[:, :sep_rows]
    if carry_ref.shape[1] > sep_rows:
        carry_ref[:, sep_rows:] = following[:, sep_rows + skipped :]


def keep_kernel(step, own_ref, received_ref, *refs):
    lower = ((lax.axis_index("leaf") >> step) & 1) == 0
    refs[-1][...] = jnp.where(lower, own_ref[...], received_ref[...])


def keep_top_kernel(step, own_ref, received_ref, passed_ref, out_ref):
    k = lax.axis_index("leaf")
    lower = ((k >> step) & 1) == 0
    near = ((k >> (step - 1)) & 1) == 0
    upper = jnp.where(near, received_ref[...], passed_ref[...])
    out_ref[...] = jnp.where(lower, own_ref[...], upper)


class Factor:
    def __init__(self, own_ref, other_ref, sep_rows, panel_rows):
        self.refs = own_ref, other_ref
        self.sep_rows, self.panel_rows = sep_rows, panel_rows
        self.half = own_ref.shape[0] - NOTE_ROWS

    def columns(self, start, size):
        own, other = (ref[: self.half, start : start + size] for ref in self.refs)
        upper = upper_part() == 1
        return jnp.concatenate([jnp.where(upper, other, own), jnp.where(upper, own, other)], axis=0)

    def inverse(self):
        return self.columns(0, self.sep_rows)

    def updates(self, count):
        return self.columns(self.sep_rows, count * self.panel_rows)

    def panel(self, index):
        start = self.sep_rows + index * self.panel_rows
        notes = self.refs[0][self.half : self.half + NOTE_ROWS, start : start + self.panel_rows]
        return notes.astype(f32)[:1]


def spread_first(message_ref, arrived_ref, wide_level, levels, sep_rows, panel_rows):
    count = sep_rows // panel_rows
    wide = message_ref[:, :sep_rows].astype(f32)
    sums = []
    for level in range(levels):
        value = wide
        panel = leaf_panel(arrived_ref, level, panel_rows)
        for a, here in ((level - 1, wide_level < level), (level, wide_level > level)):
            if 0 <= a < levels - 1:
                columns = pl.ds(sep_rows + a * panel_rows, panel_rows)
                narrow = placed(message_ref[:, columns].astype(f32), panel, count)
                value = jnp.where(here, narrow, value)
        sums.append(value)
    return sums


def solve_up(pending, factor):
    count = factor.sep_rows // factor.panel_rows
    solved = dot_t((-pending[0]).astype(bf16), factor.inverse())
    others = []
    if len(pending) > 1:
        updates = dot(solved.astype(bf16), factor.updates(len(pending) - 1))
        for a, value in enumerate(pending[1:]):
            update = updates[:, a * factor.panel_rows : (a + 1) * factor.panel_rows]
            others.append(value + placed(update, factor.panel(a), count))
    return solved, others


def sums_of(own_ref, received):
    sep_rows = received[0].shape[1]
    return [
        own_ref[:, a * sep_rows : (a + 1) * sep_rows] + value for a, value in enumerate(received)
    ]


def parts_of(ref, sep_rows):
    return [ref[:, low : low + sep_rows].astype(f32) for low in range(0, ref.shape[1], sep_rows)]


def up_kernel(levels, now, panel_rows, own_ref, received_ref, factor_ref, other_ref, *refs):
    solved_ref, sums_ref, out_ref = refs[-3:]
    sep_rows = solved_ref.shape[1]
    if now == 0:
        partner = jnp.minimum(own_level(lax.axis_index("leaf") ^ 1, levels), levels - 1)
        received = spread_first(received_ref, refs[0], partner, levels, sep_rows, panel_rows)
    else:
        received = parts_of(received_ref, sep_rows)
    factor = Factor(factor_ref, other_ref, sep_rows, panel_rows)
    solved, others = solve_up(sums_of(own_ref, received), factor)
    solved_ref[...] = solved
    for a, value in enumerate(others):
        sums_ref[:, a * sep_rows : (a + 1) * sep_rows] = value
        out_ref[:, a * sep_rows : (a + 1) * sep_rows] = value.astype(bf16)


def prepare_kernel(levels, solved_ref, update_ref, inverse_ref, base_ref, folded_ref):
    size, panel_rows = inverse_ref.shape[0], update_ref.shape[2]
    step = min(256, size)
    for low in range(0, size, step):
        high = low + step
        coarse, fine = two_parts(solved_ref[:, low:])
        block = inverse_ref[low:, low:high]
        base_ref[:, low:high] = dot(coarse, block) + dot(fine, block)
        for a in range(levels):
            folded_ref[a * panel_rows : (a + 1) * panel_rows, low:high] = contract_rows(
                update_ref[a, low:, :], block
            ).astype(bf16)


def two_parts(value):
    coarse = value.astype(bf16)
    return coarse, (value - coarse.astype(f32)).astype(bf16)


def contract_rows(a, b):
    return lax.dot_general(a, b, (((0,), (0,)), ((), ())), preferred_element_type=f32)


def fold_kernel(levels, panel_rows, *refs):
    below = levels - 1
    for now in range(below):
        own_ref, other_ref, solved_ref = refs[3 * now : 3 * now + 3]
        base_ref, folded_ref = refs[3 * below + 2 * now : 3 * below + 2 * now + 2]
        factor = Factor(own_ref, other_ref, base_ref.shape[1], panel_rows)
        inverse = factor.inverse()
        coarse, fine = two_parts(solved_ref[...])
        base_ref[...] = dot(coarse, inverse) + dot(fine, inverse)
        folded_ref[...] = contract_rows(factor.updates(below - now), inverse).astype(bf16)


def square_kernel(panel_rows, own_ref, other_ref, coarse_ref, fine_ref):
    inverse = Factor(own_ref, other_ref, coarse_ref.shape[1], panel_rows).inverse()
    coarse_ref[...], fine_ref[...] = two_parts(contract_rows(inverse, inverse))


def down_kernel(levels, *refs):
    carry_ref, own_ref, received_ref, base_ref, folded_ref, coarse_ref, fine_ref = refs[:7]
    below = levels - 1
    factor_refs = refs[7 : 7 + below]
    folds = refs[7 + below : 7 + 3 * below]
    leaf_out_hbm, sep_out_hbm, leaf_out_ref, sep_out_ref, sems = refs[7 + 3 * below :]
    level = own_level(lax.axis_index("leaf"), levels)
    sep_rows = own_ref.shape[1]
    panel_rows = folded_ref.shape[0] // levels
    count = sep_rows // panel_rows

    residual = (-(own_ref[...] + received_ref[...].astype(f32))).astype(bf16)
    solution_now = dot(residual, coarse_ref[...]) + dot(residual, fine_ref[...])
    ancestors = {below: solution_now.astype(bf16).astype(f32)}
    sep_out = jnp.where(level == below, solution_now, 0.0)
    for now in reversed(range(below)):
        factor = Factor(factor_refs[now], None, sep_rows, panel_rows)
        blocks = [
            picked(ancestors[a], factor.panel(a - now - 1), count).astype(bf16)
            for a in range(now + 1, levels)
        ]
        solution_now = folds[2 * now][...] - dot(
            jnp.concatenate(blocks, axis=1), folds[2 * now + 1][...]
        )
        ancestors[now] = solution_now.astype(bf16).astype(f32)
        sep_out = jnp.where(level == now, solution_now, sep_out)
    sep_out_ref[...] = sep_out
    leaving = [pltpu.make_async_copy(sep_out_ref, sep_out_hbm, sems.at[0])]
    leaving[0].start()

    blocks = [
        picked(ancestors[a], leaf_panel(carry_ref, a, panel_rows), count).astype(bf16)
        for a in range(levels)
    ]
    blocks = jnp.concatenate(blocks, axis=1)
    size = folded_ref.shape[1]
    step = min(256, size)
    for low in range(0, size, step):
        high = low + step
        leaf_out_ref[:, low:high] = base_ref[:, low:high] - dot(blocks, folded_ref[:, low:high])
        columns = pl.ds(low, step)
        leaving.append(
            pltpu.make_async_copy(
                leaf_out_ref.at[:, columns],
                leaf_out_hbm.at[:, columns],
                sems.at[len(leaving)],
            )
        )
        leaving[-1].start()
    for copy in leaving:
        copy.wait()


def local(
    leaf_rhs, sep_rhs, leaf_inverse, leaf_update, leaf_panel, sep_inverse, sep_update, sep_panel
):
    levels = lax.axis_size("leaf").bit_length() - 1
    sep_rows = sep_inverse.shape[0]
    scenarios, size = leaf_rhs.shape
    leaf_update, sep_update = leaf_update[0], sep_update[0]
    panel_rows = leaf_update.shape[2]
    panel_smem = pltpu.SMEM(leaf_panel.shape, jnp.int32)
    sems = pltpu.SemaphoreType.DMA((levels + 8 + 3 * (size // min(256, size)),))
    leaf_flops = 2 * scenarios * size * (size + levels * panel_rows)

    def carry_shape(now):
        width = sep_rows + (levels - 1 - now) * panel_rows
        return ((sep_rows // 2 + NOTE_ROWS, width), bf16)

    (carry,) = call(
        partial(pack_kernel, levels),
        [carry_shape(0)],
        (sep_panel, leaf_panel, sep_inverse, sep_update),
        hbm=range(4),
        scratch=[panel_smem, panel_smem, sems],
    )
    first_carry, arrived = carry, exchange(carry, 1)
    leaf_inverse, leaf_update, leaf_solved, sums, message = call(
        partial(leaf_up_kernel, levels),
        [
            (leaf_inverse.shape, bf16),
            (leaf_update.shape, bf16),
            ((scenarios, size), f32),
            ((scenarios, levels * sep_rows), f32),
            ((scenarios, sep_rows + (levels - 1) * panel_rows), bf16),
        ],
        (carry, leaf_rhs, leaf_inverse, leaf_update, sep_rhs),
        hbm=range(1, 5),
        scratch=[pltpu.VMEM(leaf_rhs.shape, bf16), pltpu.VMEM(sep_rhs.shape, bf16), sems],
        flops=leaf_flops,
    )
    received = exchange(message, 1)
    base, folded = call(
        partial(prepare_kernel, levels),
        [((scenarios, size), f32), ((levels * panel_rows, size), bf16)],
        (leaf_solved, leaf_update, leaf_inverse),
        flops=2 * leaf_flops,
    )
    first = (arrived,)
    factors, solved = [], []
    for now in range(levels):
        pair = (carry, arrived)
        if now + 1 < levels:
            (carry,) = call(
                partial(hand_on_kernel, now, sep_rows), [carry_shape(now + 1)], pair
            )
            if now + 2 < levels:
                arrived = exchange(carry, 2 << now)
            else:
                quarter = 1 << now
                arrived = exchange_among(carry, 3 * quarter, range(quarter, 3 * quarter))
                passed = exchange_among(arrived, quarter, range(2 * quarter, 4 * quarter))
            pair += (carry,)
        elif levels > 1:
            pair += (passed,)
        kernel = keep_kernel if now + 1 < levels or levels == 1 else keep_top_kernel
        factors += call(partial(kernel, now), [carry_shape(now)], pair)
        factors.append(exchange(factors[-1], 1, "rhs"))
        if now + 1 == levels:
            break
        extra = (*first, folded) if now == 0 else ()
        extra += (arrived,) if now + 2 < levels else ()
        z, sums, message = call(
            partial(up_kernel, levels, now, panel_rows),
            [
                ((scenarios, sep_rows), f32),
                ((scenarios, (levels - 1 - now) * sep_rows), f32),
                ((scenarios, (levels - 1 - now) * sep_rows), bf16),
            ],
            (sums, received, *factors[-2:], *extra),
            flops=2 * scenarios * sep_rows * sep_rows * 2,
        )
        solved.append(z)
        received = exchange(message, 2 << now)
    below = levels - 1
    triples, shapes = (), []
    for now in range(below):
        triples += (factors[2 * now], factors[2 * now + 1], solved[now])
        shapes += [((scenarios, sep_rows), f32), (((below - now) * panel_rows, sep_rows), bf16)]
    folds = call(
        partial(fold_kernel, levels, panel_rows),
        shapes,
        triples,
        flops=6 * below * scenarios * sep_rows * sep_rows,
    )
    square = call(
        partial(square_kernel, panel_rows),
        [((sep_rows, sep_rows), bf16)] * 2,
        (factors[-2], factors[-1]),
        flops=2 * sep_rows**3,
    )
    return call(
        partial(down_kernel, levels),
        [((scenarios, size), f32), ((scenarios, sep_rows), f32)],
        (first_carry, sums, received, base, folded, *square, *factors[: 2 * below : 2], *folds),
        hbm_outs=True,
        scratch=[
            pltpu.VMEM((scenarios, size), f32),
            pltpu.VMEM((scenarios, sep_rows), f32),
            sems,
        ],
        flops=leaf_flops,
    )


def solution(mesh):
    return jax.shard_map(
        local,
        mesh=mesh,
        in_specs=(
            P("rhs", "leaf"),
            P("rhs", "leaf"),
            P("leaf", None),
            P("leaf", None, None, None),
            P("leaf", None),
            P("leaf", None),
            P("leaf", None, None, None),
            P("leaf", None),
        ),
        out_specs=(P("rhs", "leaf"), P("rhs", "leaf")),
        check_vma=False,
    )
```

```python
from functools import partial

import jax
import jax.numpy as jnp
from jax import lax
from jax.experimental import pallas as pl
from jax.experimental.pallas import tpu as pltpu
from jax.sharding import PartitionSpec as P

NOTE_ROWS = 16
f32, bf16 = jnp.float32, jnp.bfloat16


def dot(a, b):
    return jnp.dot(a, b, preferred_element_type=f32)


def dot_t(a, b):
    return lax.dot_general(a, b, (((1,), (1,)), ((), ())), preferred_element_type=f32)


def own_level(k, levels):
    level = jnp.int32(0)
    for bit in range(levels):
        low = (2 << bit) - 1
        level = jnp.where((k & low) == low, bit + 1, level)
    return level


def placed(block, panel, count):
    return jnp.concatenate(
        [jnp.where(panel == p, block, jnp.zeros_like(block)) for p in range(count)], axis=1
    )


def picked(vectors, panel, count):
    width = vectors.shape[1] // count
    result = vectors[:, :width]
    for p in range(1, count):
        result = jnp.where(panel == p, vectors[:, p * width : (p + 1) * width], result)
    return result


def call(kernel, outs, args, hbm=(), hbm_outs=False, scratch=(), flops=0):
    def bytes_of(arrays):
        return sum(a.size * a.dtype.itemsize for a in arrays)

    outs = [jax.ShapeDtypeStruct(shape, dtype) for shape, dtype in outs]
    args = [
        pltpu.with_memory_space_constraint(arg, pltpu.HBM) if i in hbm else arg
        for i, arg in enumerate(args)
    ]
    return pl.pallas_call(
        kernel,
        out_shape=outs,
        in_specs=[
            pl.BlockSpec(memory_space=pltpu.HBM if i in hbm else pltpu.VMEM)
            for i in range(len(args))
        ],
        out_specs=[pl.BlockSpec(memory_space=pltpu.HBM if hbm_outs else pltpu.VMEM) for _ in outs],
        scratch_shapes=scratch,
        compiler_params=pltpu.CompilerParams(vmem_limit_bytes=40 << 20),
        cost_estimate=pl.CostEstimate(
            flops=flops, bytes_accessed=bytes_of(args) + bytes_of(outs), transcendentals=0
        ),
    )(*args)


def exchange(block, distance, axis="leaf"):
    return lax.ppermute(block, axis, [(i, i ^ distance) for i in range(lax.axis_size(axis))])


def exchange_among(block, distance, members):
    leaves, parts = lax.axis_size("leaf"), lax.axis_size("rhs")
    route = []
    for leaf in range(leaves):
        for part in range(parts):
            target = (leaf ^ distance, part) if leaf in members else (leaf, part ^ 1)
            route.append((leaf * parts + part, target[0] * parts + target[1]))
    return lax.ppermute(block, ("leaf", "rhs"), route)


def upper_part():
    return lax.axis_index("rhs") & 1


def pack_kernel(
    levels,
    sep_panel_hbm,
    leaf_panel_hbm,
    sep_inverse_hbm,
    sep_update_hbm,
    carry_ref,
    sep_panel_ref,
    leaf_panel_ref,
    sems,
):
    sep_rows, panel_rows = sep_inverse_hbm.shape[1], sep_update_hbm.shape[2]
    half = sep_rows // 2
    copies = []

    def bring(source, target):
        copies.append(pltpu.make_async_copy(source, target, sems.at[len(copies)]))
        copies[-1].start()

    bring(sep_panel_hbm, sep_panel_ref)
    bring(leaf_panel_hbm, leaf_panel_ref)
    rows = pl.ds(pl.multiple_of(upper_part() * half, half), half)
    bring(sep_inverse_hbm.at[rows], carry_ref.at[pl.ds(0, half), pl.ds(0, sep_rows)])
    for a in range(1, levels):
        columns = pl.ds(sep_rows + (a - 1) * panel_rows, panel_rows)
        bring(sep_update_hbm.at[a, rows], carry_ref.at[pl.ds(0, half), columns])

    copies[0].wait()
    copies[1].wait()
    row = lax.broadcasted_iota(jnp.int32, (NOTE_ROWS, sep_rows), 0)
    notes = jnp.zeros((NOTE_ROWS, sep_rows), f32)
    for a in range(levels):
        notes = jnp.where(row == a, leaf_panel_ref[0, a].astype(f32), notes)
    carry_ref[half:, :sep_rows] = notes.astype(bf16)
    for a in range(1, levels):
        columns = pl.ds(sep_rows + (a - 1) * panel_rows, panel_rows)
        carry_ref[half:, columns] = jnp.full(
            (NOTE_ROWS, panel_rows), sep_panel_ref[0, a].astype(f32)
        ).astype(bf16)
    for copy in copies[2:]:
        copy.wait()


def leaf_up_kernel(
    levels,
    carry_ref,
    rhs_hbm,
    inverse_hbm,
    update_hbm,
    sep_rhs_hbm,
    inverse_ref,
    update_ref,
    solved_ref,
    own_ref,
    out_ref,
    rhs_ref,
    sep_rhs_ref,
    sems,
):
    k = lax.axis_index("leaf")
    sep_rows = sep_rhs_ref.shape[1]
    size, panel_rows = inverse_ref.shape[0], update_ref.shape[2]
    count = sep_rows // panel_rows
    step = min(256, size)
    lows = range(0, size, step)
    copies = []

    def bring(source, target):
        copies.append(pltpu.make_async_copy(source, target, sems.at[len(copies)]))
        copies[-1].start()

    bring(rhs_hbm, rhs_ref)
    for low in lows:
        block = (pl.ds(low, step), pl.ds(0, low + step))
        bring(inverse_hbm.at[block], inverse_ref.at[block])
    bring(update_hbm, update_ref)
    bring(sep_rhs_hbm, sep_rhs_ref)

    def solve(low):
        high = low + step
        value = dot_t(rhs_ref[:, :high], inverse_ref[low:high, :high])
        solved_ref[:, low:high] = value
        return value.astype(bf16)

    early = len(copies) - 3
    for copy in copies[:early]:
        copy.wait()
    rounded = [solve(low) for low in lows[:-1]]
    for copy in copies[early:]:
        copy.wait()
    rounded.append(solve(lows[-1]))
    updates = jnp.concatenate([update_ref[a] for a in range(levels)], axis=1)
    together = dot(jnp.concatenate(rounded, axis=1), updates)
    terms = [together[:, a * panel_rows : (a + 1) * panel_rows] for a in range(levels)]
    level = own_level(k, levels)
    wide_level = jnp.minimum(level, levels - 1)
    rhs = jnp.where(level < levels, sep_rhs_ref[...].astype(f32), 0.0)
    wide = jnp.zeros(rhs.shape, f32)
    for a in range(levels):
        spread = placed(terms[a], leaf_panel(carry_ref, a, panel_rows), count)
        spread = jnp.where(wide_level == a, spread - rhs, spread)
        wide = jnp.where(wide_level == a, spread, wide)
        own_ref[:, a * sep_rows : (a + 1) * sep_rows] = spread
    out_ref[:, :sep_rows] = wide.astype(bf16)
    for a in range(levels - 1):
        columns = pl.ds(sep_rows + a * panel_rows, panel_rows)
        out_ref[:, columns] = jnp.where(wide_level <= a, terms[a + 1], terms[a]).astype(bf16)


def leaf_panel(first_carry_ref, level, panel_rows):
    rows = first_carry_ref.shape[0]
    notes = first_carry_ref[rows - NOTE_ROWS :, :panel_rows].astype(f32)
    return notes[level : level + 1]


def hand_on_kernel(step, sep_rows, own_ref, received_ref, carry_ref):
    lower = ((lax.axis_index("leaf") >> step) & 1) == 0
    following = jnp.where(lower, received_ref[...], own_ref[...])
    skipped = own_ref.shape[1] - carry_ref.shape[1]
    carry_ref[:, :sep_rows] = following[:, :sep_rows]
    if carry_ref.shape[1] > sep_rows:
        carry_ref[:, sep_rows:] = following[:, sep_rows + skipped :]


def keep_kernel(step, own_ref, received_ref, *refs):
    lower = ((lax.axis_index("leaf") >> step) & 1) == 0
    refs[-1][...] = jnp.where(lower, own_ref[...], received_ref[...])


def keep_top_kernel(step, own_ref, received_ref, passed_ref, out_ref):
    k = lax.axis_index("leaf")
    lower = ((k >> step) & 1) == 0
    near = ((k >> (step - 1)) & 1) == 0
    upper = jnp.where(near, received_ref[...], passed_ref[...])
    out_ref[...] = jnp.where(lower, own_ref[...], upper)


class Factor:
    def __init__(self, own_ref, other_ref, sep_rows, panel_rows):
        self.refs = own_ref, other_ref
        self.sep_rows, self.panel_rows = sep_rows, panel_rows
        self.half = own_ref.shape[0] - NOTE_ROWS

    def columns(self, start, size):
        own, other = (ref[: self.half, start : start + size] for ref in self.refs)
        upper = upper_part() == 1
        return jnp.concatenate([jnp.where(upper, other, own), jnp.where(upper, own, other)], axis=0)

    def inverse(self):
        return self.columns(0, self.sep_rows)

    def updates(self, count):
        return self.columns(self.sep_rows, count * self.panel_rows)

    def panel(self, index):
        start = self.sep_rows + index * self.panel_rows
        notes = self.refs[0][self.half : self.half + NOTE_ROWS, start : start + self.panel_rows]
        return notes.astype(f32)[:1]


def spread_first(message_ref, arrived_ref, wide_level, levels, sep_rows, panel_rows):
    count = sep_rows // panel_rows
    wide = message_ref[:, :sep_rows].astype(f32)
    sums = []
    for level in range(levels):
        value = wide
        panel = leaf_panel(arrived_ref, level, panel_rows)
        for a, here in ((level - 1, wide_level < level), (level, wide_level > level)):
            if 0 <= a < levels - 1:
                columns = pl.ds(sep_rows + a * panel_rows, panel_rows)
                narrow = placed(message_ref[:, columns].astype(f32), panel, count)
                value = jnp.where(here, narrow, value)
        sums.append(value)
    return sums


def solve_up(pending, factor):
    count = factor.sep_rows // factor.panel_rows
    solved = dot_t((-pending[0]).astype(bf16), factor.inverse())
    others = []
    if len(pending) > 1:
        updates = dot(solved.astype(bf16), factor.updates(len(pending) - 1))
        for a, value in enumerate(pending[1:]):
            update = updates[:, a * factor.panel_rows : (a + 1) * factor.panel_rows]
            others.append(value + placed(update, factor.panel(a), count))
    return solved, others


def sums_of(own_ref, received):
    sep_rows = received[0].shape[1]
    return [
        own_ref[:, a * sep_rows : (a + 1) * sep_rows] + value for a, value in enumerate(received)
    ]


def parts_of(ref, sep_rows):
    return [ref[:, low : low + sep_rows].astype(f32) for low in range(0, ref.shape[1], sep_rows)]


def up_kernel(levels, now, panel_rows, own_ref, received_ref, factor_ref, other_ref, *refs):
    solved_ref, sums_ref, out_ref = refs[-3:]
    sep_rows = solved_ref.shape[1]
    if now == 0:
        partner = jnp.minimum(own_level(lax.axis_index("leaf") ^ 1, levels), levels - 1)
        received = spread_first(received_ref, refs[0], partner, levels, sep_rows, panel_rows)
    else:
        received = parts_of(received_ref, sep_rows)
    factor = Factor(factor_ref, other_ref, sep_rows, panel_rows)
    solved, others = solve_up(sums_of(own_ref, received), factor)
    solved_ref[...] = solved
    for a, value in enumerate(others):
        sums_ref[:, a * sep_rows : (a + 1) * sep_rows] = value
        out_ref[:, a * sep_rows : (a + 1) * sep_rows] = value.astype(bf16)


def prepare_kernel(levels, solved_ref, update_ref, inverse_ref, base_ref, folded_ref):
    size, panel_rows = inverse_ref.shape[0], update_ref.shape[2]
    step = min(256, size)
    for low in range(0, size, step):
        high = low + step
        coarse, fine = two_parts(solved_ref[:, low:])
        block = inverse_ref[low:, low:high]
        base_ref[:, low:high] = dot(coarse, block) + dot(fine, block)
        for a in range(levels):
            folded_ref[a * panel_rows : (a + 1) * panel_rows, low:high] = contract_rows(
                update_ref[a, low:, :], block
            ).astype(bf16)


def two_parts(value):
    coarse = value.astype(bf16)
    return coarse, (value - coarse.astype(f32)).astype(bf16)


def contract_rows(a, b):
    return lax.dot_general(a, b, (((0,), (0,)), ((), ())), preferred_element_type=f32)


def fold_kernel(levels, panel_rows, *refs):
    below = levels - 1
    for now in range(below):
        own_ref, other_ref, solved_ref = refs[3 * now : 3 * now + 3]
        base_ref, folded_ref = refs[3 * below + 2 * now : 3 * below + 2 * now + 2]
        factor = Factor(own_ref, other_ref, base_ref.shape[1], panel_rows)
        inverse = factor.inverse()
        coarse, fine = two_parts(solved_ref[...])
        base_ref[...] = dot(coarse, inverse) + dot(fine, inverse)
        folded_ref[...] = contract_rows(factor.updates(below - now), inverse).astype(bf16)


def square_kernel(panel_rows, own_ref, other_ref, coarse_ref, fine_ref):
    inverse = Factor(own_ref, other_ref, coarse_ref.shape[1], panel_rows).inverse()
    coarse_ref[...], fine_ref[...] = two_parts(contract_rows(inverse, inverse))


def down_kernel(levels, *refs):
    carry_ref, own_ref, received_ref, base_ref, folded_ref, coarse_ref, fine_ref = refs[:7]
    below = levels - 1
    factor_refs = refs[7 : 7 + below]
    folds = refs[7 + below : 7 + 3 * below]
    leaf_out_hbm, sep_out_hbm, leaf_out_ref, sep_out_ref, sems = refs[7 + 3 * below :]
    level = own_level(lax.axis_index("leaf"), levels)
    sep_rows = own_ref.shape[1]
    panel_rows = folded_ref.shape[0] // levels
    count = sep_rows // panel_rows

    residual = (-(own_ref[...] + received_ref[...].astype(f32))).astype(bf16)
    solution_now = dot(residual, coarse_ref[...]) + dot(residual, fine_ref[...])
    ancestors = {below: solution_now.astype(bf16).astype(f32)}
    sep_out = jnp.where(level == below, solution_now, 0.0)
    for now in reversed(range(below)):
        factor = Factor(factor_refs[now], None, sep_rows, panel_rows)
        blocks = [
            picked(ancestors[a], factor.panel(a - now - 1), count).astype(bf16)
            for a in range(now + 1, levels)
        ]
        solution_now = folds[2 * now][...] - dot(
            jnp.concatenate(blocks, axis=1), folds[2 * now + 1][...]
        )
        ancestors[now] = solution_now.astype(bf16).astype(f32)
        sep_out = jnp.where(level == now, solution_now, sep_out)
    sep_out_ref[...] = sep_out
    leaving = [pltpu.make_async_copy(sep_out_ref, sep_out_hbm, sems.at[0])]
    leaving[0].start()

    blocks = [
        picked(ancestors[a], leaf_panel(carry_ref, a, panel_rows), count).astype(bf16)
        for a in range(levels)
    ]
    blocks = jnp.concatenate(blocks, axis=1)
    size = folded_ref.shape[1]
    step = min(256, size)
    for low in range(0, size, step):
        high = low + step
        leaf_out_ref[:, low:high] = base_ref[:, low:high] - dot(blocks, folded_ref[:, low:high])
        columns = pl.ds(low, step)
        leaving.append(
            pltpu.make_async_copy(
                leaf_out_ref.at[:, columns],
                leaf_out_hbm.at[:, columns],
                sems.at[len(leaving)],
            )
        )
        leaving[-1].start()
    for copy in leaving:
        copy.wait()


def local(
    leaf_rhs, sep_rhs, leaf_inverse, leaf_update, leaf_panel, sep_inverse, sep_update, sep_panel
):
    levels = lax.axis_size("leaf").bit_length() - 1
    sep_rows = sep_inverse.shape[0]
    scenarios, size = leaf_rhs.shape
    leaf_update, sep_update = leaf_update[0], sep_update[0]
    panel_rows = leaf_update.shape[2]
    panel_smem = pltpu.SMEM(leaf_panel.shape, jnp.int32)
    sems = pltpu.SemaphoreType.DMA((levels + 8 + 3 * (size // min(256, size)),))
    leaf_flops = 2 * scenarios * size * (size + levels * panel_rows)

    def carry_shape(now):
        width = sep_rows + (levels - 1 - now) * panel_rows
        return ((sep_rows // 2 + NOTE_ROWS, width), bf16)

    (carry,) = call(
        partial(pack_kernel, levels),
        [carry_shape(0)],
        (sep_panel, leaf_panel, sep_inverse, sep_update),
        hbm=range(4),
        scratch=[panel_smem, panel_smem, sems],
    )
    first_carry, arrived = carry, exchange(carry, 1)
    leaf_inverse, leaf_update, leaf_solved, sums, message = call(
        partial(leaf_up_kernel, levels),
        [
            (leaf_inverse.shape, bf16),
            (leaf_update.shape, bf16),
            ((scenarios, size), f32),
            ((scenarios, levels * sep_rows), f32),
            ((scenarios, sep_rows + (levels - 1) * panel_rows), bf16),
        ],
        (carry, leaf_rhs, leaf_inverse, leaf_update, sep_rhs),
        hbm=range(1, 5),
        scratch=[pltpu.VMEM(leaf_rhs.shape, bf16), pltpu.VMEM(sep_rhs.shape, bf16), sems],
        flops=leaf_flops,
    )
    received = exchange(message, 1)
    base, folded = call(
        partial(prepare_kernel, levels),
        [((scenarios, size), f32), ((levels * panel_rows, size), bf16)],
        (leaf_solved, leaf_update, leaf_inverse),
        flops=2 * leaf_flops,
    )
    first = (arrived,)
    factors, solved = [], []
    for now in range(levels):
        pair = (carry, arrived)
        if now + 1 < levels:
            (carry,) = call(
                partial(hand_on_kernel, now, sep_rows), [carry_shape(now + 1)], pair
            )
            if now + 2 < levels:
                arrived = exchange(carry, 2 << now)
            else:
                quarter = 1 << now
                arrived = exchange_among(carry, 3 * quarter, range(quarter, 3 * quarter))
                passed = exchange_among(arrived, quarter, range(2 * quarter, 4 * quarter))
            pair += (carry,)
        elif levels > 1:
            pair += (passed,)
        kernel = keep_kernel if now + 1 < levels or levels == 1 else keep_top_kernel
        factors += call(partial(kernel, now), [carry_shape(now)], pair)
        factors.append(exchange(factors[-1], 1, "rhs"))
        if now + 1 == levels:
            break
        extra = (*first, folded) if now == 0 else ()
        extra += (arrived,) if now + 2 < levels else ()
        z, sums, message = call(
            partial(up_kernel, levels, now, panel_rows),
            [
                ((scenarios, sep_rows), f32),
                ((scenarios, (levels - 1 - now) * sep_rows), f32),
                ((scenarios, (levels - 1 - now) * sep_rows), bf16),
            ],
            (sums, received, *factors[-2:], *extra),
            flops=2 * scenarios * sep_rows * sep_rows * 2,
        )
        solved.append(z)
        received = exchange(message, (3 if now + 2 == levels else 2) << now)
    below = levels - 1
    triples, shapes = (), []
    for now in range(below):
        triples += (factors[2 * now], factors[2 * now + 1], solved[now])
        shapes += [((scenarios, sep_rows), f32), (((below - now) * panel_rows, sep_rows), bf16)]
    folds = call(
        partial(fold_kernel, levels, panel_rows),
        shapes,
        triples,
        flops=6 * below * scenarios * sep_rows * sep_rows,
    )
    square = call(
        partial(square_kernel, panel_rows),
        [((sep_rows, sep_rows), bf16)] * 2,
        (factors[-2], factors[-1]),
        flops=2 * sep_rows**3,
    )
    return call(
        partial(down_kernel, levels),
        [((scenarios, size), f32), ((scenarios, sep_rows), f32)],
        (first_carry, sums, received, base, folded, *square, *factors[: 2 * below : 2], *folds),
        hbm_outs=True,
        scratch=[
            pltpu.VMEM((scenarios, size), f32),
            pltpu.VMEM((scenarios, sep_rows), f32),
            sems,
        ],
        flops=leaf_flops,
    )


def solution(mesh):
    return jax.shard_map(
        local,
        mesh=mesh,
        in_specs=(
            P("rhs", "leaf"),
            P("rhs", "leaf"),
            P("leaf", None),
            P("leaf", None, None, None),
            P("leaf", None),
            P("leaf", None),
            P("leaf", None, None, None),
            P("leaf", None),
        ),
        out_specs=(P("rhs", "leaf"), P("rhs", "leaf")),
        check_vma=False,
    )
```
